32 devices in a mesh: groups: 2 (over y), node: 4 (over z), local: 4 (over x, core).
Axes of the slice: x: 2, y: 2, z: 4, core: 2. Of those that a mesh axis runs over, the one named last changes fastest.
Arguments:
- tokens: bfloat16 [4096, 3584], P(('groups', 'node', 'local')), parts along dimension 0, may hold values from -6 to 6
- routing_gate_weight: float32 [4096, 8], P(('groups', 'node', 'local')), parts along dimension 0, may hold values from 0.1 to 0.5
- selected_expert_index: int32 [4096, 8], P(('groups', 'node', 'local')), parts along dimension 0, may hold values from 0 to 31, as said below
- w_gate: bfloat16 [4, 3584, 1024], P('node', None, 'local'), may hold values from -0.09375 to 0.09375
- w_up: bfloat16 [4, 3584, 1024], P('node', None, 'local'), may hold values from -0.09375 to 0.09375
- w_down: bfloat16 [4, 1024, 3584], P('node', 'local'), may hold values from -0.1875 to 0.1875
- s_gate: bfloat16 [3584, 1024], P(None, 'local'), may hold values from -0.09375 to 0.09375
- s_up: bfloat16 [3584, 1024], P(None, 'local'), may hold values from -0.09375 to 0.09375
- s_down: bfloat16 [1024, 3584], P('local'), may hold values from -0.1875 to 0.1875
Outputs:
- mixed: bfloat16 [4096, 3584], P(('groups', 'node', 'local')), parts along dimension 0
The draws below stay inside these ranges and needn't reach their ends.
There are 2 independent parts, one for each index of `groups`. The reference program is written for one: setup_inputs(seed, part) draws one part's arguments, and reference() takes and returns one part's arrays. A program takes and returns all parts, laid end to end along the dimension named above; an argument that names none is the same for every part. Nothing has to cross between parts.
Inputs may be any that keep to these rules, and one draw needn't show every extreme that they name: `selected_expert_index`: expert e belongs to node e // 8. A token's 8 experts are two distinct experts in each of 4 distinct nodes. Among the tokens of one device at most 8 name the in-flight expert of any one node, and for one node, the same for every device of a part, the in-flight expert is named by exactly 8 tokens of every device; the other nodes' in-flight experts are named by at most 8.
All inputs are finite; a program needn't handle non-finite values.
Results may differ from the reference program's by a relative error of at most 0.0095.
Values may be sent and summed in bfloat16 or wider, within the bound.
No kernel may reach another device: no remote copies, remote signals or barrier semaphores. Data moves between devices by JAX's collectives and lax.ppermute only.
A program may use at most 128 MiB of HBM per device.

```python
import jax
import jax.numpy as jnp
from jax import lax

D = 3584
FFW = 1024
SFF = 1024
TOPK = 8
NODESET = 4
EXPERTS_PER_NODE = 8
TOK_DEV = 128
CAP = 8
TOKENS = 2048
N_NODE = 4
N_LOCAL = 4


def draw_selected_expert_index(key, part):
    key = jax.random.fold_in(key, 7)
    subkeys = jax.random.split(key, 6)
    blocks = N_NODE * N_LOCAL
    node_range = jnp.arange(N_NODE, dtype=jnp.int32)
    hot_node = jax.random.randint(subkeys[0], (), 0, N_NODE, dtype=jnp.int32)
    scores = jax.random.randint(subkeys[1], (blocks, TOK_DEV, N_NODE), 0, 1 << 16, dtype=jnp.int32) * N_NODE + node_range
    scores = jnp.where(node_range == hot_node, -1, scores)
    _, others = lax.top_k(scores, NODESET - 1)
    others = others.astype(jnp.int32)
    order_keys = jax.random.randint(subkeys[2], (blocks, TOK_DEV), 0, 1 << 16, dtype=jnp.int32) * TOK_DEV + jnp.arange(TOK_DEV, dtype=jnp.int32)
    rank_order = jnp.argsort(jnp.argsort(order_keys, axis=1), axis=1)
    hot_hit = rank_order < CAP
    wanted = jax.random.randint(subkeys[3], (blocks, TOK_DEV, NODESET - 1), 0, 3, dtype=jnp.int32) == 0
    onehot = ((others[..., None] == node_range) & wanted[..., None]).astype(jnp.int32)
    per_node = jnp.sum(onehot, axis=2)
    before = jnp.cumsum(per_node, axis=1) - per_node
    earlier = jnp.take_along_axis(before, others, axis=2)
    other_hit = wanted & (earlier < CAP)
    node_set = jnp.concatenate([jnp.broadcast_to(hot_node, (blocks, TOK_DEV, 1)), others], axis=2)
    hit_flags = jnp.concatenate([hot_hit[..., None], other_hit], axis=2)
    first_pick = jax.random.randint(subkeys[4], (blocks, TOK_DEV, NODESET), 1, EXPERTS_PER_NODE, dtype=jnp.int32)
    step_pick = jax.random.randint(subkeys[5], (blocks, TOK_DEV, NODESET), 1, EXPERTS_PER_NODE - 1, dtype=jnp.int32)
    second_pick = 1 + (first_pick - 1 + step_pick) % (EXPERTS_PER_NODE - 1)
    low_pick = jnp.where(hit_flags, 0, first_pick)
    high_pick = jnp.where(hit_flags, first_pick, second_pick)
    offset = node_set * EXPERTS_PER_NODE
    chosen_ids = jnp.stack([offset + low_pick, offset + high_pick], axis=3)
    return chosen_ids.reshape(TOKENS, TOPK).astype(jnp.int32)


def block_scale(key, shape, shards, smallest, high):
    factor_of = 1.0
    for dim, blocks in shards:
        draws = jax.random.uniform(jax.random.fold_in(jax.random.fold_in(key, 6), dim), (blocks,), jnp.float32, smallest / len(shards), high / len(shards))
        factor_of = factor_of * jnp.repeat(jnp.exp(draws), shape[dim] // blocks).reshape((-1,) + (1,) * (len(shape) - 1 - dim))
    return factor_of


def scatter_about(stream_key, dims, width, reach, cuts=(), kind=jnp.bfloat16):
    values = width * jax.random.normal(stream_key, dims, jnp.float32)
    if cuts:
        values = values * block_scale(stream_key, dims, cuts, -0.22, 0.18)
    return jnp.clip(values, -reach, reach).astype(kind)


def setup_inputs(seed: int = 0, part: int = 0) -> dict:
    keys = jax.random.split(jax.random.key(seed), 10)
    part_splits = jax.random.split(jax.random.fold_in(keys[9], part), 10)
    tokens = scatter_about(part_splits[0], (TOKENS, D), 1.0, 6.0, ((0, 16),))
    routing_gate_weight = jnp.clip(0.1 + 0.4 * jax.random.uniform(part_splits[1], (TOKENS, TOPK), jnp.float32) ** block_scale(part_splits[1], (TOKENS, TOPK), ((0, 16),), -0.2, 0.2), 0.1, 0.5)
    selected_expert_index = draw_selected_expert_index(jax.random.fold_in(jax.random.fold_in(keys[9], part), 71), part)
    w_gate = scatter_about(keys[3], (N_NODE, D, FFW), D ** -0.5, 0.09375, ((0, 4), (2, 4)))
    w_up = scatter_about(keys[4], (N_NODE, D, FFW), D ** -0.5, 0.09375, ((0, 4), (2, 4)))
    w_down = scatter_about(keys[5], (N_NODE, FFW, D), FFW ** -0.5, 0.1875, ((0, 4), (1, 4)))
    s_gate = scatter_about(keys[6], (D, SFF), D ** -0.5, 0.09375, ((1, 4),))
    s_up = scatter_about(keys[7], (D, SFF), D ** -0.5, 0.09375, ((1, 4),))
    s_down = scatter_about(keys[8], (SFF, D), SFF ** -0.5, 0.1875, ((0, 4),))
    return {"tokens": tokens, "routing_gate_weight": routing_gate_weight, "selected_expert_index": selected_expert_index, "w_gate": w_gate, "w_up": w_up, "w_down": w_down, "s_gate": s_gate, "s_up": s_up, "s_down": s_down}


def quarter_sum(hidden, w_down):
    slice_size = w_down.shape[0] // N_LOCAL
    summed = jnp.zeros((hidden.shape[0], w_down.shape[1]), jnp.float32)
    for quarter in range(N_LOCAL):
        piece_out = jnp.dot(hidden[:, quarter * slice_size:(quarter + 1) * slice_size],
                            w_down[quarter * slice_size:(quarter + 1) * slice_size],
                            preferred_element_type=jnp.float32).astype(jnp.bfloat16)
        piece_out = lax.optimization_barrier(piece_out)
        summed = summed + piece_out.astype(jnp.float32)
    return summed


def expert_rows(row_block, w_gate, w_up, w_down):
    gate = jnp.dot(row_block, w_gate, preferred_element_type=jnp.float32)
    lifted = jnp.dot(row_block, w_up, preferred_element_type=jnp.float32)
    hidden = (jax.nn.silu(gate) * lifted).astype(jnp.bfloat16)
    return quarter_sum(hidden, w_down)


def reference(tokens, routing_gate_weight, selected_expert_index, w_gate, w_up, w_down, s_gate, s_up, s_down):
    rows_max = N_NODE * N_LOCAL * CAP
    row_index = jnp.arange(TOKENS, dtype=jnp.int32)

    def one_node(routed_sum, node_id):
        owner_id = node_id * EXPERTS_PER_NODE
        matched = selected_expert_index == owner_id
        weight = jnp.sum(jnp.where(matched, routing_gate_weight, jnp.float32(0.0)), axis=1)
        chosen = jnp.any(matched, axis=1)
        sort_key = jnp.where(chosen, row_index, row_index + TOKENS)
        picked = jnp.argsort(sort_key)[:rows_max].astype(jnp.int32)
        row_block = tokens[picked]
        result = expert_rows(row_block, w_gate[node_id], w_up[node_id], w_down[node_id]).astype(jnp.bfloat16)
        result = lax.optimization_barrier(result)
        capacity_factor = weight[picked]
        routed_sum = routed_sum.at[picked].add(capacity_factor[:, None] * result.astype(jnp.float32))
        return routed_sum, None

    routed, _ = lax.scan(one_node, jnp.zeros((TOKENS, D), jnp.float32), jnp.arange(N_NODE, dtype=jnp.int32))
    shared = expert_rows(tokens, s_gate, s_up, s_down)
    return (shared + routed).astype(jnp.bfloat16)
```

```python
import jax
import jax.numpy as jnp
from jax import lax
from jax.experimental import pallas as pl
from jax.experimental.pallas import tpu as pltpu
from jax.sharding import PartitionSpec as P

EXPERTS_PER_NODE = 8
CHUNKS = 2
FEW_NODES = 8


def shift(value, axis, mask):
    size = lax.axis_size(axis)
    return lax.ppermute(value, axis, [(i, i ^ mask) for i in range(size)])


def dispatch_kernel(node_count, capacity, owner_ref, index_ref, gate_ref, tokens_ref, rows_ref, weight_ref):
    count = index_ref.shape[1]
    index = index_ref[...]
    gates = gate_ref[...]
    before = lax.broadcasted_iota(jnp.int32, (count, count), 0)
    after = lax.broadcasted_iota(jnp.int32, (count, count), 1)
    earlier = (before < after).astype(jnp.bfloat16)
    chosen, weights = [], []
    for n in range(node_count):
        match = index == owner_ref[n]
        chosen.append(jnp.max(match.astype(jnp.float32), axis=0, keepdims=True))
        weights.append(jnp.sum(jnp.where(match, gates, 0.0), axis=0, keepdims=True))
    chosen = jnp.concatenate(chosen, axis=0)
    position = jnp.dot(chosen.astype(jnp.bfloat16), earlier, preferred_element_type=jnp.float32)
    slot = lax.broadcasted_iota(jnp.int32, (capacity, count), 0).astype(jnp.float32)
    picks, scaled = [], []
    for n in range(node_count):
        hit = (position[n : n + 1] == slot) & (chosen[n : n + 1] > 0.5)
        picks.append(hit.astype(jnp.float32))
        scaled.append(jnp.where(hit, weights[n], 0.0))
    pick = jnp.concatenate(picks, axis=0).astype(jnp.bfloat16)
    rows_ref[...] = jnp.dot(pick, tokens_ref[...], preferred_element_type=jnp.float32).astype(
        jnp.bfloat16
    )
    weight_ref[...] = jnp.concatenate(scaled, axis=0)


def dispatch(node_count, capacity, index, gates, tokens):
    count, width = tokens.shape
    slots = node_count * capacity
    vmem = pl.BlockSpec(memory_space=pltpu.VMEM)
    nodes = jnp.arange(node_count, dtype=jnp.int32)
    if node_count <= FEW_NODES:
        nodes = nodes ^ lax.axis_index("node")
    return pl.pallas_call(
        lambda *refs: dispatch_kernel(node_count, capacity, *refs),
        out_shape=(
            jax.ShapeDtypeStruct((slots, width), jnp.bfloat16),
            jax.ShapeDtypeStruct((slots, count), jnp.float32),
        ),
        in_specs=[pl.BlockSpec(memory_space=pltpu.SMEM), vmem, vmem, vmem],
        out_specs=(vmem, vmem),
        compiler_params=pltpu.CompilerParams(vmem_limit_bytes=32 * 1024 * 1024),
    )(nodes * EXPERTS_PER_NODE, index.T, gates.T, tokens)


def dot(a, b):
    return jnp.dot(a, b, preferred_element_type=jnp.float32)


def hidden_of(rows, gate, up):
    return (jax.nn.silu(dot(rows, gate)) * dot(rows, up)).astype(jnp.bfloat16)


def over_nodes(blocks):
    if blocks.shape[0] > FEW_NODES:
        return lax.all_to_all(blocks, "node", split_axis=0, concat_axis=0, tiled=True)
    return jnp.stack([shift(blocks[m], "node", m) if m else blocks[0] for m in range(len(blocks))])


def per_device(
    tokens, routing_gate_weight, selected_expert_index, w_gate, w_up, w_down, s_gate, s_up, s_down
):
    node_count = lax.axis_size("node")
    count, width = tokens.shape
    capacity = count // 16
    slots = node_count * capacity

    step = count // CHUNKS
    afar = [shift(tokens[i * step : (i + 1) * step], "local", 2) for i in range(CHUNKS)]
    p_gate, p_up, p_down = (shift(w, "local", 1) for w in (s_gate, s_up, s_down))

    outgoing, weight = dispatch(
        node_count, capacity, selected_expert_index, routing_gate_weight, tokens
    )
    near = over_nodes(outgoing.reshape(node_count, capacity, width)).reshape(slots, width)
    far = shift(near, "local", 2)
    pair = jnp.concatenate([near, far], axis=0)
    every = jnp.concatenate([pair, shift(pair, "local", 1)], axis=0)
    part = dot(hidden_of(every, w_gate[0], w_up[0]), w_down[0])
    mine, other = part[: 2 * slots], part[2 * slots :].astype(jnp.bfloat16)
    chip = mine + shift(other, "local", 1).astype(jnp.float32)
    crossing = shift(chip[slots:].astype(jnp.bfloat16), "local", 2)
    summed = (chip[:slots] + crossing.astype(jnp.float32)).astype(jnp.bfloat16)
    replies = over_nodes(summed.reshape(node_count, capacity, width)).reshape(slots, width)

    def shared_part(rows):
        return dot(hidden_of(rows, s_gate, s_up), s_down) + dot(
            hidden_of(rows, p_gate, p_up), p_down
        )

    own = shared_part(tokens)
    back = [shift(shared_part(rows).astype(jnp.bfloat16), "local", 2) for rows in afar]
    shared = own + jnp.concatenate(back, axis=0).astype(jnp.float32)

    high = weight.astype(jnp.bfloat16)
    low = (weight - high.astype(jnp.float32)).astype(jnp.bfloat16)
    both = jnp.concatenate([high, low], axis=0)
    twice = jnp.concatenate([replies, replies], axis=0)
    routed = lax.dot_general(
        both, twice, (((0,), (0,)), ((), ())), preferred_element_type=jnp.float32
    )
    return (shared + routed).astype(jnp.bfloat16)


def solution(mesh):
    in_specs = (
        P(("groups", "node", "local"), None),
        P(("groups", "node", "local"), None),
        P(("groups", "node", "local"), None),
        P("node", None, "local"),
        P("node", None, "local"),
        P("node", "local", None),
        P(None, "local"),
        P(None, "local"),
        P("local", None),
    )
    out_specs = P(("groups", "node", "local"), None)
    return jax.shard_map(
        per_device, mesh=mesh, in_specs=in_specs, out_specs=out_specs, check_vma=False
    )
```

```python
import jax
import jax.numpy as jnp
from jax import lax
from jax.experimental import pallas as pl
from jax.experimental.pallas import tpu as pltpu
from jax.sharding import PartitionSpec as P

EXPERTS_PER_NODE = 8
FEW_NODES = 8
PIECES = 4
HBM = pl.BlockSpec(memory_space=pltpu.HBM)
VMEM = pl.BlockSpec(memory_space=pltpu.VMEM)
SMEM = pl.BlockSpec(memory_space=pltpu.SMEM)
ROWS = (((0,), (0,)), ((), ()))
COLS = (((1,), (1,)), ((), ()))


def shift(value, axis, mask):
    size = lax.axis_size(axis)
    return lax.ppermute(value, axis, [(i, i ^ mask) for i in range(size)])


def over_nodes(pieces):
    count = len(pieces)
    if count > FEW_NODES:
        moved = lax.all_to_all(jnp.stack(pieces), "node", split_axis=0, concat_axis=0, tiled=True)
        return [moved[n] for n in range(count)]
    return [shift(piece, "node", m) if m else piece for m, piece in enumerate(pieces)]


def dot(a, b, dims=(((1,), (0,)), ((), ()))):
    return lax.dot_general(a, b, dims, preferred_element_type=jnp.float32)


def bf16(value):
    return value.astype(jnp.bfloat16)


def struct(rows, cols, dtype=jnp.bfloat16):
    return jax.ShapeDtypeStruct((rows, cols), dtype)


def call(kernel, outs, args, specs=None, scratch=(), room=0, flops=0):
    return pl.pallas_call(
        kernel,
        out_shape=outs,
        in_specs=specs or [VMEM] * len(args),
        out_specs=jax.tree.map(lambda _: VMEM, outs),
        scratch_shapes=scratch,
        cost_estimate=pl.CostEstimate(flops=flops, bytes_accessed=0, transcendentals=0),
        compiler_params=pltpu.CompilerParams(vmem_limit_bytes=(8 << 20) + room),
    )(*args)


def head_kernel(
    nodes, block, owner_ref, index_hbm, gate_hbm, tokens_hbm,
    first_ref, mix_ref, pick_ref, tokens_ref, index_ref, gate_ref, sems,
):
    copies = [
        pltpu.make_async_copy(index_hbm, index_ref, sems.at[0]),
        pltpu.make_async_copy(gate_hbm, gate_ref, sems.at[1]),
        pltpu.make_async_copy(tokens_hbm, tokens_ref, sems.at[2]),
    ]
    for copy in copies:
        copy.start()
    count, width = tokens_ref.shape
    head = first_ref.shape[0]
    row = lax.broadcasted_iota(jnp.int32, (count, count), 0)
    col = lax.broadcasted_iota(jnp.int32, (count, count), 1)
    earlier = bf16((row < col).astype(jnp.float32))
    copies[0].wait()
    copies[1].wait()
    index = index_ref[...]
    gates = gate_ref[...]
    chosen, weights = [], []
    for n in range(nodes):
        match = index == owner_ref[n]
        chosen.append(jnp.max(match.astype(jnp.float32), axis=0, keepdims=True))
        weights.append(jnp.sum(jnp.where(match, gates, 0.0), axis=0, keepdims=True))
    wanted = jnp.max(jnp.concatenate(chosen, axis=0), axis=0, keepdims=True)
    flags = jnp.concatenate(chosen + [wanted] + [jnp.zeros_like(wanted)] * (-(nodes + 1) % 8), axis=0)
    position = dot(bf16(flags), earlier)
    ahead = position[nodes : nodes + 1]
    total = jnp.sum(wanted)
    place = lax.broadcasted_iota(jnp.int32, (1, count), 1).astype(jnp.float32)
    rank = jnp.where(wanted > 0.5, ahead, total + place - ahead)
    order = bf16((rank == row.astype(jnp.float32)).astype(jnp.float32))
    slot = lax.broadcasted_iota(jnp.int32, (block, count), 0).astype(jnp.float32)
    picks, own, other = [], [], []
    for n in range(nodes):
        here = (position[n : n + 1] == slot) & (chosen[n] > 0.5)
        there = (position[n : n + 1] + block // 2 == slot) & (chosen[n] > 0.5)
        picks.append(here.astype(jnp.float32))
        own.append(jnp.where(here, weights[n], 0.0))
        other.append(jnp.where(there, weights[n], 0.0))
    own = jnp.concatenate(own, axis=0)
    other = jnp.concatenate(other, axis=0)
    own_high, other_high = bf16(own), bf16(other)
    own_low = bf16(own - own_high.astype(jnp.float32))
    other_low = bf16(other - other_high.astype(jnp.float32))
    slots = nodes * block
    mix_ref[:count] = order
    mix_ref[count : count + slots] = own_high
    mix_ref[count + slots :] = own_low
    pick_ref[...] = bf16(jnp.concatenate(picks, axis=0))
    first_ref[:, width : width + slots] = bf16(dot(order[:head], other_high, COLS))
    first_ref[:, width + slots :] = bf16(dot(order[:head], other_low, COLS))
    copies[2].wait()
    first_ref[:, :width] = bf16(dot(order[:head], tokens_ref[...]))


def tail_kernel(head, mix_ref, pick_ref, tokens_ref, near_ref, rest_ref=None):
    tokens = tokens_ref[...]
    if rest_ref is not None:
        rest_ref[...] = bf16(dot(mix_ref[head : tokens_ref.shape[0]], tokens))
    near_ref[...] = bf16(dot(pick_ref[...], tokens))


def join_kernel(block, near_ref, first_ref, *outs):
    slots, width = near_ref.shape
    high = first_ref[:, width : width + slots].astype(jnp.float32)
    pick = bf16((high != 0.0).astype(jnp.float32))
    far = dot(pick, first_ref[:, :width], ROWS)
    both = near_ref[...].astype(jnp.float32) + far
    for n, out in enumerate(outs):
        out[...] = bf16(both[n * block : (n + 1) * block])


def mlp(rows, gate, up, down):
    v = dot(rows, gate[...])
    hidden = bf16(v / (1.0 + jnp.exp(-v)) * dot(rows, up[...]))
    return dot(hidden, down[...])


def expert_kernel(nodes, *refs):
    rows = [r[...] for r in refs[:nodes]]
    mats, outs = refs[nodes : nodes + 6], refs[nodes + 6 :]
    block = rows[0].shape[0]
    rows = jnp.concatenate(rows, axis=0)
    part = mlp(rows, *mats[:3]) + mlp(rows, *mats[3:])
    for n, out in enumerate(outs):
        out[...] = bf16(part[n * block : (n + 1) * block])


def own_kernel(
    tokens_ref, gate, up, down, sg_hbm, su_hbm, sd_hbm, wg_hbm, wu_hbm, wd_hbm,
    own_ref, sg, su, sd, wg, wu, wd, sems,
):
    pairs = zip((sg_hbm, su_hbm, sd_hbm, wg_hbm, wu_hbm, wd_hbm), (sg, su, sd, wg, wu, wd))
    copies = [pltpu.make_async_copy(a, b, sems.at[i]) for i, (a, b) in enumerate(pairs)]
    for copy in copies:
        copy.start()
    rows = tokens_ref[...]
    own_ref[...] = mlp(rows, gate, up, down)
    for copy in copies[:3]:
        copy.wait()
    own_ref[...] += mlp(rows, sg, su, sd)
    for copy in copies[3:]:
        copy.wait()


def far_kernel(groups, *refs):
    ins, mats, outs = refs[:groups], refs[groups : groups + 6], refs[groups + 6 :]
    rows = jnp.concatenate([r[:, : outs[0].shape[1]] for r in ins], axis=0)
    sums = mlp(rows, *mats[:3]) + mlp(rows, *mats[3:])
    start = 0
    for out in outs:
        out[...] = sums[start : start + out.shape[0]].astype(out.dtype)
        start += out.shape[0]


def fold_kernel(part_ref, first_ref, *refs):
    width = part_ref.shape[1]
    replies = jnp.concatenate([r[...] for r in refs[:-1]], axis=0)
    slots = replies.shape[0]
    high = first_ref[:, width : width + slots]
    low = first_ref[:, width + slots :]
    refs[-1][...] = bf16(part_ref[...] + dot(high, replies) + dot(low, replies))


def final_kernel(back_count, *refs):
    own_ref, mix_ref = refs[:2]
    backs, replies = refs[2 : 2 + back_count], refs[2 + back_count : -3]
    out_hbm, out_ref, sems = refs[-3:]
    width = out_ref.shape[1]
    tile = width // PIECES
    copies = []
    for i in range(PIECES):
        cols = slice(i * tile, (i + 1) * tile)
        reply = [r[:, cols] for r in replies]
        terms = jnp.concatenate([*[r[:, cols] for r in backs], *reply, *reply], axis=0)
        out_ref[:, cols] = bf16(own_ref[:, cols] + dot(mix_ref[...], terms, ROWS))
        copies.append(pltpu.make_async_copy(out_ref.at[:, cols], out_hbm.at[:, cols], sems.at[i]))
        copies[-1].start()
    for copy in copies:
        copy.wait()


def per_device(
    tokens, routing_gate_weight, selected_expert_index, w_gate, w_up, w_down, s_gate, s_up, s_down
):
    nodes = lax.axis_size("node")
    count, width = tokens.shape
    capacity = count // 16
    block = 2 * capacity
    slots = nodes * block
    head = min(nodes * capacity, count)
    tail = count - head

    owners = jnp.arange(nodes, dtype=jnp.int32)
    if nodes <= FEW_NODES:
        owners = owners ^ lax.axis_index("node")
    topk = selected_expert_index.shape[1]
    first, mix, pick, held = call(
        lambda *refs: head_kernel(nodes, block, *refs),
        (
            struct(head, width + 2 * slots),
            struct(count + 2 * slots, count),
            struct(slots, count),
            struct(count, width),
        ),
        (owners * EXPERTS_PER_NODE, selected_expert_index.T, routing_gate_weight.T, tokens),
        specs=[SMEM, HBM, HBM, HBM],
        scratch=[
            pltpu.VMEM((topk, count), jnp.int32),
            pltpu.VMEM((topk, count), jnp.float32),
            pltpu.SemaphoreType.DMA((3,)),
        ],
        room=4 * slots * width,
    )
    far_first = shift(first, "local", 2)
    near, *rest = call(
        lambda *refs: tail_kernel(head, *refs),
        [struct(slots, width)] + [struct(tail, width)] * (tail > 0),
        (mix, pick, held),
        room=4 * (slots + count) * width,
    )
    far = [far_first] + [shift(r, "local", 2) for r in rest]
    shared_mats = (s_gate, s_up, s_down)
    shared_far = [shift(w, "local", 1) for w in shared_mats]
    routed_mats = (w_gate[0], w_up[0], w_down[0])
    routed_far = [shift(w, "local", 1) for w in routed_mats]

    own, *mats = call(
        own_kernel,
        [
            struct(count, width, jnp.float32),
            *[struct(*w.shape) for w in shared_mats],
            *[struct(*w.shape) for w in routed_mats],
        ],
        (held, *shared_far, *shared_mats, *routed_mats),
        specs=[VMEM] * 4 + [HBM] * 6,
        scratch=[pltpu.SemaphoreType.DMA((6,))],
        room=12 * count * width,
        flops=30 * count * width * s_gate.shape[1],
    )
    sent = call(
        lambda *refs: join_kernel(block, *refs),
        [struct(block, width)] * nodes,
        (near, far_first),
        room=8 * slots * width,
    )
    arrived = over_nodes(sent)
    replied = call(
        lambda *refs: expert_kernel(nodes, *refs),
        [struct(block, width)] * nodes,
        (*arrived, *routed_far, *mats[3:]),
        room=12 * slots * width,
        flops=40 * slots * width * w_gate.shape[2],
    )
    replies = over_nodes(replied)
    part, *sums = call(
        lambda *refs: far_kernel(len(far), *refs),
        [struct(head, width, jnp.float32)] + [struct(tail, width)] * len(rest),
        (*far, *shared_far, *mats[:3]),
        room=12 * count * width,
        flops=24 * count * width * s_gate.shape[1],
    )
    late = [shift(r, "local", 2) for r in sums]
    folded = call(
        fold_kernel,
        struct(head, width),
        (part, far_first, *replies),
        room=8 * slots * width,
    )
    backs = [shift(folded, "local", 2)] + late
    return pl.pallas_call(
        lambda *refs: final_kernel(len(backs), *refs),
        out_shape=struct(count, width),
        in_specs=[VMEM] * (2 + len(backs) + nodes),
        out_specs=HBM,
        scratch_shapes=[
            pltpu.VMEM((count, width), jnp.bfloat16),
            pltpu.SemaphoreType.DMA((PIECES,)),
        ],
        compiler_params=pltpu.CompilerParams(vmem_limit_bytes=(8 << 20) + 8 * slots * width),
    )(own, mix, *backs, *replies)


def solution(mesh):
    in_specs = (
        P(("groups", "node", "local"), None),
        P(("groups", "node", "local"), None),
        P(("groups", "node", "local"), None),
        P("node", None, "local"),
        P("node", None, "local"),
        P("node", "local", None),
        P(None, "local"),
        P(None, "local"),
        P("local", None),
    )
    out_specs = P(("groups", "node", "local"), None)
    return jax.shard_map(
        per_device, mesh=mesh, in_specs=in_specs, out_specs=out_specs, check_vma=False
    )
```

```python
import jax
import jax.numpy as jnp
from jax import lax
from jax.experimental import pallas as pl
from jax.experimental.pallas import tpu as pltpu
from jax.sharding import PartitionSpec as P

EXPERTS_PER_NODE = 8
FEW_NODES = 8
COST = {"head": 3000000000, "tail": 100000000, "load": 100000000000, "join": 1000000000, "own": 3000000000, "expert": 100000000, "far": 100000000000, "fold": 3000000000, "final": 100000000000}
PIECES = 4
HBM = pl.BlockSpec(memory_space=pltpu.HBM)
VMEM = pl.BlockSpec(memory_space=pltpu.VMEM)
SMEM = pl.BlockSpec(memory_space=pltpu.SMEM)
ROWS = (((0,), (0,)), ((), ()))
COLS = (((1,), (1,)), ((), ()))


def shift(value, axis, mask):
    size = lax.axis_size(axis)
    return lax.ppermute(value, axis, [(i, i ^ mask) for i in range(size)])


def over_nodes(pieces):
    count = len(pieces)
    if count > FEW_NODES:
        moved = lax.all_to_all(jnp.stack(pieces), "node", split_axis=0, concat_axis=0, tiled=True)
        return [moved[n] for n in range(count)]
    return [shift(piece, "node", m) if m else piece for m, piece in enumerate(pieces)]


def dot(a, b, dims=(((1,), (0,)), ((), ()))):
    return lax.dot_general(a, b, dims, preferred_element_type=jnp.float32)


def bf16(value):
    return value.astype(jnp.bfloat16)


def struct(rows, cols, dtype=jnp.bfloat16):
    return jax.ShapeDtypeStruct((rows, cols), dtype)


def call(name, kernel, outs, args, specs=None, scratch=(), room=0, limit=0):
    if specs:
        args = [
            pltpu.with_memory_space_constraint(a, pltpu.HBM) if s is HBM else a
            for a, s in zip(args, specs)
        ]
    return pl.pallas_call(
        kernel,
        name="scope_" + name,
        out_shape=outs,
        in_specs=specs or [VMEM] * len(args),
        out_specs=jax.tree.map(lambda _: VMEM, outs),
        scratch_shapes=scratch,
        cost_estimate=pl.CostEstimate(flops=COST[name], bytes_accessed=0, transcendentals=0),
        compiler_params=pltpu.CompilerParams(vmem_limit_bytes=limit or (8 << 20) + room),
    )(*args)


def head_kernel(
    nodes, block, owner_ref, index_hbm, gate_hbm, tokens_hbm,
    first_ref, mix_ref, pick_ref, tokens_ref, index_ref, gate_ref, sems,
):
    copies = [
        pltpu.make_async_copy(index_hbm, index_ref, sems.at[0]),
        pltpu.make_async_copy(gate_hbm, gate_ref, sems.at[1]),
        pltpu.make_async_copy(tokens_hbm, tokens_ref, sems.at[2]),
    ]
    for copy in copies:
        copy.start()
    count, width = tokens_ref.shape
    head = first_ref.shape[0]
    row = lax.broadcasted_iota(jnp.int32, (count, count), 0)
    col = lax.broadcasted_iota(jnp.int32, (count, count), 1)
    earlier = bf16((row < col).astype(jnp.float32))
    copies[0].wait()
    copies[1].wait()
    index = index_ref[...]
    gates = gate_ref[...]
    chosen, weights = [], []
    for n in range(nodes):
        match = index == owner_ref[n]
        chosen.append(jnp.max(match.astype(jnp.float32), axis=0, keepdims=True))
        weights.append(jnp.sum(jnp.where(match, gates, 0.0), axis=0, keepdims=True))
    wanted = jnp.max(jnp.concatenate(chosen, axis=0), axis=0, keepdims=True)
    flags = jnp.concatenate(chosen + [wanted] + [jnp.zeros_like(wanted)] * (-(nodes + 1) % 8), axis=0)
    position = dot(bf16(flags), earlier)
    ahead = position[nodes : nodes + 1]
    total = jnp.sum(wanted)
    place = lax.broadcasted_iota(jnp.int32, (1, count), 1).astype(jnp.float32)
    rank = jnp.where(wanted > 0.5, ahead, total + place - ahead)
    order = bf16((rank == row.astype(jnp.float32)).astype(jnp.float32))
    slot = lax.broadcasted_iota(jnp.int32, (block, count), 0).astype(jnp.float32)
    picks, own, other = [], [], []
    for n in range(nodes):
        here = (position[n : n + 1] == slot) & (chosen[n] > 0.5)
        there = (position[n : n + 1] + block // 2 == slot) & (chosen[n] > 0.5)
        picks.append(here.astype(jnp.float32))
        own.append(jnp.where(here, weights[n], 0.0))
        other.append(jnp.where(there, weights[n], 0.0))
    own = jnp.concatenate(own, axis=0)
    other = jnp.concatenate(other, axis=0)
    own_high, other_high = bf16(own), bf16(other)
    own_low = bf16(own - own_high.astype(jnp.float32))
    other_low = bf16(other - other_high.astype(jnp.float32))
    slots = nodes * block
    mix_ref[:count] = order
    mix_ref[count : count + slots] = own_high
    mix_ref[count + slots :] = own_low
    pick_ref[...] = bf16(jnp.concatenate(picks, axis=0))
    first_ref[:, width : width + slots] = bf16(dot(order[:head], other_high, COLS))
    first_ref[:, width + slots :] = bf16(dot(order[:head], other_low, COLS))
    copies[2].wait()
    first_ref[:, :width] = bf16(dot(order[:head], tokens_ref[...]))


def tail_kernel(head, mix_ref, pick_ref, tokens_ref, near_ref, rest_ref=None):
    tokens = tokens_ref[...]
    if rest_ref is not None:
        rest_ref[...] = bf16(dot(mix_ref[head : tokens_ref.shape[0]], tokens))
    near_ref[...] = bf16(dot(pick_ref[...], tokens))


def join_kernel(block, near_ref, first_ref, *outs):
    slots, width = near_ref.shape
    high = first_ref[:, width : width + slots].astype(jnp.float32)
    pick = bf16((high != 0.0).astype(jnp.float32))
    far = dot(pick, first_ref[:, :width], ROWS)
    both = near_ref[...].astype(jnp.float32) + far
    for n, out in enumerate(outs):
        out[...] = bf16(both[n * block : (n + 1) * block])


def mlp(rows, gate, up, down):
    v = dot(rows, gate[...])
    hidden = bf16(v / (1.0 + jnp.exp(-v)) * dot(rows, up[...]))
    return dot(hidden, down[...])


def load_kernel(gate_hbm, up_hbm, down_hbm, near_ref, pack_ref, sems):
    width, part = gate_hbm.shape
    copies = [(gate_hbm, 0), (up_hbm, width)]
    copies += [(down_hbm.at[:, i : i + part], 2 * width + i) for i in range(0, width, part)]
    copies = [
        pltpu.make_async_copy(
            source, pack_ref.at[place : place + source.shape[0]], sems.at[i]
        )
        for i, (source, place) in enumerate(copies)
    ]
    for copy in copies:
        copy.start()
    for copy in copies:
        copy.wait()


def expert_kernel(nodes, *refs):
    rows = [r[...] for r in refs[:nodes]]
    packs, outs = refs[nodes : nodes + 2], refs[nodes + 2 :]
    block, width = rows[0].shape
    part = packs[0].shape[1]
    rows = jnp.concatenate(rows, axis=0)
    hidden = []
    for pack in packs:
        v = dot(rows, pack[:width])
        hidden.append(bf16(v / (1.0 + jnp.exp(-v)) * dot(rows, pack[width : 2 * width])))
    for i in range(0, width, part):
        down = slice(2 * width + i, 2 * width + i + part)
        sums = dot(hidden[0], packs[0][down]) + dot(hidden[1], packs[1][down])
        for n, out in enumerate(outs):
            out[:, i : i + part] = bf16(sums[n * block : (n + 1) * block])


def own_kernel(
    tokens_ref, gate, up, down, after_ref, sg_hbm, su_hbm, sd_hbm, own_ref, sg, su, sd, sems,
):
    pairs = zip((sg_hbm, su_hbm, sd_hbm), (sg, su, sd))
    copies = [pltpu.make_async_copy(a, b, sems.at[i]) for i, (a, b) in enumerate(pairs)]
    for copy in copies:
        copy.start()
    rows = tokens_ref[...]
    own_ref[...] = mlp(rows, gate, up, down)
    for copy in copies:
        copy.wait()
    own_ref[...] += mlp(rows, sg, su, sd)


def far_kernel(groups, *refs):
    ins, mats, outs = refs[:groups], refs[groups : groups + 6], refs[groups + 6 :]
    rows = jnp.concatenate([r[:, : outs[0].shape[1]] for r in ins], axis=0)
    sums = mlp(rows, *mats[:3]) + mlp(rows, *mats[3:])
    start = 0
    for out in outs:
        out[...] = sums[start : start + out.shape[0]].astype(out.dtype)
        start += out.shape[0]


def fold_kernel(part_ref, first_ref, *refs):
    width = part_ref.shape[1]
    replies = jnp.concatenate([r[...] for r in refs[:-1]], axis=0)
    slots = replies.shape[0]
    high = first_ref[:, width : width + slots]
    low = first_ref[:, width + slots :]
    refs[-1][...] = bf16(part_ref[...] + dot(high, replies) + dot(low, replies))


def final_kernel(back_count, *refs):
    own_ref, mix_ref = refs[:2]
    backs, replies = refs[2 : 2 + back_count], refs[2 + back_count : -3]
    out_hbm, out_ref, sems = refs[-3:]
    width = out_ref.shape[1]
    tile = width // PIECES
    copies = []
    for i in range(PIECES):
        cols = slice(i * tile, (i + 1) * tile)
        reply = [r[:, cols] for r in replies]
        terms = jnp.concatenate([*[r[:, cols] for r in backs], *reply, *reply], axis=0)
        out_ref[:, cols] = bf16(own_ref[:, cols] + dot(mix_ref[...], terms, ROWS))
        copies.append(pltpu.make_async_copy(out_ref.at[:, cols], out_hbm.at[:, cols], sems.at[i]))
        copies[-1].start()
    for copy in copies:
        copy.wait()


def per_device(
    tokens, routing_gate_weight, selected_expert_index, w_gate, w_up, w_down, s_gate, s_up, s_down
):
    nodes = lax.axis_size("node")
    count, width = tokens.shape
    capacity = count // 16
    block = 2 * capacity
    slots = nodes * block
    head = min(nodes * capacity, count)
    tail = count - head

    owners = jnp.arange(nodes, dtype=jnp.int32)
    if nodes <= FEW_NODES:
        owners = owners ^ lax.axis_index("node")
    topk = selected_expert_index.shape[1]
    first, mix, pick, held = call(
        "head",
        lambda *refs: head_kernel(nodes, block, *refs),
        (
            struct(head, width + 2 * slots),
            struct(count + 2 * slots, count),
            struct(slots, count),
            struct(count, width),
        ),
        (owners * EXPERTS_PER_NODE, selected_expert_index.T, routing_gate_weight.T, tokens),
        specs=[SMEM, HBM, HBM, HBM],
        scratch=[
            pltpu.VMEM((topk, count), jnp.int32),
            pltpu.VMEM((topk, count), jnp.float32),
            pltpu.SemaphoreType.DMA((3,)),
        ],
        limit=16 << 20,
    )
    far_first = shift(first, "local", 2)
    near, *rest = call(
        "tail",
        lambda *refs: tail_kernel(head, *refs),
        [struct(slots, width)] + [struct(tail, width)] * (tail > 0),
        (mix, pick, held),
        room=4 * (slots + count) * width,
    )
    far = [far_first] + [shift(r, "local", 2) for r in rest]
    shared_mats = (s_gate, s_up, s_down)
    shared_far = [shift(w, "local", 1) for w in shared_mats]
    sent = call(
        "join",
        lambda *refs: join_kernel(block, *refs),
        [struct(block, width)] * nodes,
        (near, far_first),
        room=8 * slots * width,
    )
    part = w_gate.shape[2]
    pack = call(
        "load",
        load_kernel,
        struct(3 * width, part),
        (w_gate[0], w_up[0], w_down[0], sent[0]),
        specs=[HBM] * 3 + [VMEM],
        scratch=[pltpu.SemaphoreType.DMA((2 + width // part,))],
        limit=16 << 20,
    )
    far_pack = shift(pack, "local", 1)
    arrived = over_nodes(sent)
    own, *mats = call(
        "own",
        own_kernel,
        [
            struct(count, width, jnp.float32),
            *[struct(*w.shape) for w in shared_mats],
        ],
        (held, *shared_far, near, *shared_mats),
        specs=[VMEM] * 5 + [HBM] * 3,
        scratch=[pltpu.SemaphoreType.DMA((3,))],
        limit=16 << 20,
    )
    replied = call(
        "expert",
        lambda *refs: expert_kernel(nodes, *refs),
        [struct(block, width)] * nodes,
        (*arrived, pack, far_pack),
        room=20 * slots * width + (4 << 20),
    )
    replies = over_nodes(replied)
    sums_first, *sums = call(
        "far",
        lambda *refs: far_kernel(len(far), *refs),
        [struct(head, width, jnp.float32)] + [struct(tail, width)] * len(rest),
        (*far, *shared_far, *mats),
        room=12 * count * width,
    )
    late = [shift(r, "local", 2) for r in sums]
    folded = call(
        "fold",
        fold_kernel,
        struct(head, width),
        (sums_first, far_first, *replies),
        room=8 * slots * width,
    )
    backs = [shift(folded, "local", 2)] + late
    return pl.pallas_call(
        lambda *refs: final_kernel(len(backs), *refs),
        name="scope_final",
        out_shape=struct(count, width),
        in_specs=[VMEM] * (2 + len(backs) + nodes),
        out_specs=HBM,
        scratch_shapes=[
            pltpu.VMEM((count, width), jnp.bfloat16),
            pltpu.SemaphoreType.DMA((PIECES,)),
        ],
        cost_estimate=pl.CostEstimate(flops=COST["final"], bytes_accessed=0, transcendentals=0),
        compiler_params=pltpu.CompilerParams(vmem_limit_bytes=(8 << 20) + 8 * slots * width),
    )(own, mix, *backs, *replies)


def solution(mesh):
    in_specs = (
        P(("groups", "node", "local"), None),
        P(("groups", "node", "local"), None),
        P(("groups", "node", "local"), None),
        P("node", None, "local"),
        P("node", None, "local"),
        P("node", "local", None),
        P(None, "local"),
        P(None, "local"),
        P("local", None),
    )
    out_specs = P(("groups", "node", "local"), None)
    return jax.shard_map(
        per_device, mesh=mesh, in_specs=in_specs, out_specs=out_specs, check_vma=False
    )
```

```python
import jax
import jax.numpy as jnp
from jax import lax
from jax.experimental import pallas as pl
from jax.experimental.pallas import tpu as pltpu
from jax.sharding import PartitionSpec as P

EXPERTS_PER_NODE = 8
FEW_NODES = 8
COST = {"head": 100000000, "tail": 3000000000, "load": 30000000000, "join": 30000000000, "own": 100000000, "expert": 30000000000, "far0": 1, "far1": 10000000000, "fold": 1000000000, "final": 10000000000, "last": 30000000000}
PIECES = 4
HBM = pl.BlockSpec(memory_space=pltpu.HBM)
VMEM = pl.BlockSpec(memory_space=pltpu.VMEM)
SMEM = pl.BlockSpec(memory_space=pltpu.SMEM)
ROWS = (((0,), (0,)), ((), ()))
COLS = (((1,), (1,)), ((), ()))


def shift(value, axis, mask):
    size = lax.axis_size(axis)
    return lax.ppermute(value, axis, [(i, i ^ mask) for i in range(size)])


def over_nodes(pieces, known=()):
    count = len(pieces)
    known = known or [None] * count
    if count > FEW_NODES:
        moved = lax.all_to_all(jnp.stack(pieces), "node", split_axis=0, concat_axis=0, tiled=True)
        return [moved[n] for n in range(count)]
    moved = list(pieces)
    for m in range(count - 1, 0, -1):
        moved[m] = shift(pieces[m], "node", m) if known[m] is None else known[m]
    return moved


def dot(a, b, dims=(((1,), (0,)), ((), ()))):
    return lax.dot_general(a, b, dims, preferred_element_type=jnp.float32)


def bf16(value):
    return value.astype(jnp.bfloat16)


def struct(rows, cols, dtype=jnp.bfloat16):
    return jax.ShapeDtypeStruct((rows, cols), dtype)


def call(name, kernel, outs, args, specs=None, scratch=(), room=0, limit=0):
    if specs:
        args = [
            pltpu.with_memory_space_constraint(a, pltpu.HBM) if s is HBM else a
            for a, s in zip(args, specs)
        ]
    return pl.pallas_call(
        kernel,
        name="scope_" + name,
        out_shape=outs,
        in_specs=specs or [VMEM] * len(args),
        out_specs=jax.tree.map(lambda _: VMEM, outs),
        scratch_shapes=scratch,
        cost_estimate=pl.CostEstimate(flops=COST[name], bytes_accessed=0, transcendentals=0),
        compiler_params=pltpu.CompilerParams(vmem_limit_bytes=limit or (8 << 20) + room),
    )(*args)


def head_kernel(
    nodes, block, owner_ref, index_hbm, gate_hbm, tokens_hbm,
    first_ref, mix_ref, pick_ref, tokens_ref, index_ref, gate_ref, sems,
):
    copies = [
        pltpu.make_async_copy(index_hbm, index_ref, sems.at[0]),
        pltpu.make_async_copy(gate_hbm, gate_ref, sems.at[1]),
        pltpu.make_async_copy(tokens_hbm, tokens_ref, sems.at[2]),
    ]
    for copy in copies:
        copy.start()
    count, width = tokens_ref.shape
    head = first_ref.shape[0]
    row = lax.broadcasted_iota(jnp.int32, (count, count), 0)
    col = lax.broadcasted_iota(jnp.int32, (count, count), 1)
    earlier = bf16((row < col).astype(jnp.float32))
    copies[0].wait()
    copies[1].wait()
    index = index_ref[...]
    gates = gate_ref[...]
    chosen, weights = [], []
    for n in range(nodes):
        match = index == owner_ref[n]
        chosen.append(jnp.max(match.astype(jnp.float32), axis=0, keepdims=True))
        weights.append(jnp.sum(jnp.where(match, gates, 0.0), axis=0, keepdims=True))
    wanted = jnp.max(jnp.concatenate(chosen, axis=0), axis=0, keepdims=True)
    flags = jnp.concatenate(chosen + [wanted] + [jnp.zeros_like(wanted)] * (-(nodes + 1) % 8), axis=0)
    position = dot(bf16(flags), earlier)
    ahead = position[nodes : nodes + 1]
    total = jnp.sum(wanted)
    place = lax.broadcasted_iota(jnp.int32, (1, count), 1).astype(jnp.float32)
    rank = jnp.where(wanted > 0.5, ahead, total + place - ahead)
    order = bf16((rank == row.astype(jnp.float32)).astype(jnp.float32))
    slot = lax.broadcasted_iota(jnp.int32, (block, count), 0).astype(jnp.float32)
    picks, own, other = [], [], []
    for n in range(nodes):
        here = (position[n : n + 1] == slot) & (chosen[n] > 0.5)
        there = (position[n : n + 1] + block // 2 == slot) & (chosen[n] > 0.5)
        picks.append(here.astype(jnp.float32))
        own.append(jnp.where(here, weights[n], 0.0))
        other.append(jnp.where(there, weights[n], 0.0))
    own = jnp.concatenate(own, axis=0)
    other = jnp.concatenate(other, axis=0)
    own_high, other_high = bf16(own), bf16(other)
    own_low = bf16(own - own_high.astype(jnp.float32))
    other_low = bf16(other - other_high.astype(jnp.float32))
    slots = nodes * block
    mix_ref[:count] = order
    mix_ref[count : count + slots] = own_high
    mix_ref[count + slots :] = own_low
    pick_ref[...] = bf16(jnp.concatenate(picks, axis=0))
    first_ref[:, width : width + slots] = bf16(dot(order[:head], other_high, COLS))
    first_ref[:, width + slots :] = bf16(dot(order[:head], other_low, COLS))
    copies[2].wait()
    first_ref[:, :width] = bf16(dot(order[:head], tokens_ref[...]))


def tail_kernel(head, mix_ref, pick_ref, tokens_ref, near_ref, *rest):
    tokens = tokens_ref[...]
    for out in rest:
        out[...] = bf16(dot(mix_ref[head : head + out.shape[0]], tokens))
        head += out.shape[0]
    near_ref[...] = bf16(dot(pick_ref[...], tokens))


def last_kernel(start, mix_ref, tokens_ref, after_ref, out_ref):
    out_ref[...] = bf16(dot(mix_ref[start : start + out_ref.shape[0]], tokens_ref[...]))


def join_kernel(nodes, block, near_ref, first_ref, *outs):
    outs = outs[-nodes:]
    slots, width = near_ref.shape
    high = first_ref[:, width : width + slots].astype(jnp.float32)
    pick = bf16((high != 0.0).astype(jnp.float32))
    far = dot(pick, first_ref[:, :width], ROWS)
    both = near_ref[...].astype(jnp.float32) + far
    for n, out in enumerate(outs):
        out[...] = bf16(both[n * block : (n + 1) * block])


def mlp(rows, gate, up, down):
    v = dot(rows, gate[...])
    hidden = bf16(v / (1.0 + jnp.exp(-v)) * dot(rows, up[...]))
    return dot(hidden, down[...])


def load_kernel(gate_hbm, up_hbm, down_hbm, near_ref, pack_ref, sems):
    width, part = gate_hbm.shape
    copies = [(gate_hbm, 0), (up_hbm, width)]
    copies += [(down_hbm.at[:, i : i + part], 2 * width + i) for i in range(0, width, part)]
    copies = [
        pltpu.make_async_copy(
            source, pack_ref.at[place : place + source.shape[0]], sems.at[i]
        )
        for i, (source, place) in enumerate(copies)
    ]
    for copy in copies:
        copy.start()
    for copy in copies:
        copy.wait()


def expert_kernel(nodes, *refs):
    rows = [r[...] for r in refs[:nodes]]
    packs, outs = refs[nodes : nodes + 2], refs[nodes + 2 :]
    block, width = rows[0].shape
    half = block // 2
    part = packs[0].shape[1]
    rows = jnp.concatenate(rows, axis=0)
    hidden = []
    for pack in packs:
        v = dot(rows, pack[:width])
        hidden.append(bf16(v / (1.0 + jnp.exp(-v)) * dot(rows, pack[width : 2 * width])))
    for i in range(0, width, part):
        down = slice(2 * width + i, 2 * width + i + part)
        sums = dot(hidden[0], packs[0][down]) + dot(hidden[1], packs[1][down])
        start = 0
        for out in outs:
            size = out.shape[0]
            out[:, i : i + part] = bf16(sums[start : start + size])
            start += size


def blocks_of(refs, block, cols=slice(None)):
    pieces = []
    for r in refs:
        piece = r[:, cols].astype(jnp.float32)
        pieces += [piece] * (block // piece.shape[0])
    return bf16(jnp.concatenate(pieces, axis=0))


def own_kernel(
    tokens_ref, gate, up, down, after_ref, sg_hbm, su_hbm, sd_hbm, own_ref, sg, su, sd, sems,
):
    pairs = zip((sg_hbm, su_hbm, sd_hbm), (sg, su, sd))
    copies = [pltpu.make_async_copy(a, b, sems.at[i]) for i, (a, b) in enumerate(pairs)]
    for copy in copies:
        copy.start()
    rows = tokens_ref[...]
    own_ref[...] = mlp(rows, gate, up, down)
    for copy in copies:
        copy.wait()
    own_ref[...] += mlp(rows, sg, su, sd)


def far_kernel(groups, *refs):
    ins, mats, outs = refs[:groups], refs[groups : groups + 6], refs[groups + 6 :]
    rows = jnp.concatenate([r[:, : outs[0].shape[1]] for r in ins], axis=0)
    sums = mlp(rows, *mats[:3]) + mlp(rows, *mats[3:])
    start = 0
    for out in outs:
        out[...] = sums[start : start + out.shape[0]].astype(out.dtype)
        start += out.shape[0]


def fold_kernel(block, part_ref, first_ref, *refs):
    width = part_ref.shape[1]
    replies = blocks_of(refs[:-1], block)
    slots = replies.shape[0]
    high = first_ref[:, width : width + slots]
    low = first_ref[:, width + slots :]
    refs[-1][...] = bf16(part_ref[...] + dot(high, replies) + dot(low, replies))


def final_kernel(block, back_count, *refs):
    own_ref, mix_ref = refs[:2]
    backs, replies = refs[2 : 2 + back_count], refs[2 + back_count : -3]
    out_hbm, out_ref, sems = refs[-3:]
    width = out_ref.shape[1]
    tile = width // PIECES
    copies = []
    for i in range(PIECES):
        cols = slice(i * tile, (i + 1) * tile)
        reply = blocks_of(replies, block, cols)
        terms = jnp.concatenate([*[r[:, cols] for r in backs], reply, reply], axis=0)
        out_ref[:, cols] = bf16(own_ref[:, cols] + dot(mix_ref[...], terms, ROWS))
        copies.append(pltpu.make_async_copy(out_ref.at[:, cols], out_hbm.at[:, cols], sems.at[i]))
        copies[-1].start()
    for copy in copies:
        copy.wait()


def per_device(
    tokens, routing_gate_weight, selected_expert_index, w_gate, w_up, w_down, s_gate, s_up, s_down
):
    nodes = lax.axis_size("node")
    count, width = tokens.shape
    capacity = count // 16
    block = 2 * capacity
    slots = nodes * block
    head = min(nodes * capacity, count)
    tail = count - head

    owners = jnp.arange(nodes, dtype=jnp.int32)
    if nodes <= FEW_NODES:
        owners = owners ^ lax.axis_index("node")
    topk = selected_expert_index.shape[1]
    first, mix, pick, held = call(
        "head",
        lambda *refs: head_kernel(nodes, block, *refs),
        (
            struct(head, width + 2 * slots),
            struct(count + 2 * slots, count),
            struct(slots, count),
            struct(count, width),
        ),
        (owners * EXPERTS_PER_NODE, selected_expert_index.T, routing_gate_weight.T, tokens),
        specs=[SMEM, HBM, HBM, HBM],
        scratch=[
            pltpu.VMEM((topk, count), jnp.int32),
            pltpu.VMEM((topk, count), jnp.float32),
            pltpu.SemaphoreType.DMA((3,)),
        ],
        limit=16 << 20,
    )
    far_first = shift(first, "local", 2)
    cut = tail * 2 // 3 // 16 * 16
    near, *rest = call(
        "tail",
        lambda *refs: tail_kernel(head, *refs),
        [struct(slots, width)] + [struct(cut, width)] * (cut > 0),
        (mix, pick, held),
        room=4 * (slots + count) * width,
    )
    rest_far = [shift(r, "local", 2) for r in rest]
    shared_mats = (s_gate, s_up, s_down)
    shared_far = [shift(w, "local", 1) for w in shared_mats]
    sent = call(
        "join",
        lambda *refs: join_kernel(nodes, block, *refs),
        [struct(block, width)] * nodes,
        (near, far_first, *[]),
        room=8 * slots * width,
    )
    part = w_gate.shape[2]
    pack = call(
        "load",
        load_kernel,
        struct(3 * width, part),
        (w_gate[0], w_up[0], w_down[0], first),
        specs=[HBM] * 3 + [VMEM],
        scratch=[pltpu.SemaphoreType.DMA((2 + width // part,))],
        limit=16 << 20,
    )
    far_pack = shift(pack, "local", 1)
    arrived = over_nodes(sent)
    if tail > cut:
        last = call(
            "last",
            lambda *refs: last_kernel(head + cut, *refs),
            struct(tail - cut, width),
            (mix, held, sent[0]),
            room=4 * count * width,
        )
        rest_far.append(shift(last, "local", 2))
    own, *mats = call(
        "own",
        own_kernel,
        [
            struct(count, width, jnp.float32),
            *[struct(*w.shape) for w in shared_mats],
        ],
        (held, *shared_far, near, *shared_mats),
        specs=[VMEM] * 5 + [HBM] * 3,
        scratch=[pltpu.SemaphoreType.DMA((3,))],
        limit=16 << 20,
    )
    whole = [n == 1 and nodes <= FEW_NODES for n in range(nodes)]
    replied = call(
        "expert",
        lambda *refs: expert_kernel(nodes, *refs),
        [
            struct(rows, width)
            for n in range(nodes)
            for rows in ([block] if whole[n] else [capacity] * 2)
        ],
        (*arrived, pack, far_pack),
        room=20 * slots * width + (4 << 20),
    )
    split = iter(replied)
    pairs = [[next(split)] if w else [next(split), next(split)] for w in whole]
    far_replies = over_nodes([p[-1] for p in pairs])
    replies = over_nodes([p[0] for p in pairs], [f if w else None for f, w in zip(far_replies, whole)])

    sums, late = [], []
    for i, rows in enumerate(([far_first] + rest_far[:1], rest_far[1:])):
        if rows:
            sums += call(
                "far" + str(i),
                lambda *refs, n=len(rows): far_kernel(n, *refs),
                [
                    struct(r.shape[0], width, jnp.float32 if r is far_first else jnp.bfloat16)
                    for r in rows
                ],
                (*rows, *shared_far, *mats),
                room=12 * count * width,
            )
    late = [shift(r, "local", 2) for r in sums[1:]]
    folded = call(
        "fold",
        lambda *refs: fold_kernel(block, *refs),
        struct(head, width),
        (sums[0], far_first, *far_replies),
        room=8 * slots * width,
    )
    backs = [shift(folded, "local", 2)] + late
    return pl.pallas_call(
        lambda *refs: final_kernel(block, len(backs), *refs),
        name="scope_final",
        out_shape=struct(count, width),
        in_specs=[VMEM] * (2 + len(backs) + nodes),
        out_specs=HBM,
        scratch_shapes=[
            pltpu.VMEM((count, width), jnp.bfloat16),
            pltpu.SemaphoreType.DMA((PIECES,)),
        ],
        cost_estimate=pl.CostEstimate(flops=COST["final"], bytes_accessed=0, transcendentals=0),
        compiler_params=pltpu.CompilerParams(vmem_limit_bytes=(8 << 20) + 8 * slots * width),
    )(own, mix, *backs, *replies)


def solution(mesh):
    in_specs = (
        P(("groups", "node", "local"), None),
        P(("groups", "node", "local"), None),
        P(("groups", "node", "local"), None),
        P("node", None, "local"),
        P("node", None, "local"),
        P("node", "local", None),
        P(None, "local"),
        P(None, "local"),
        P("local", None),
    )
    out_specs = P(("groups", "node", "local"), None)
    return jax.shard_map(
        per_device, mesh=mesh, in_specs=in_specs, out_specs=out_specs, check_vma=False
    )
```

```python
import jax
import jax.numpy as jnp
from jax import lax
from jax.experimental import pallas as pl
from jax.experimental.pallas import tpu as pltpu
from jax.sharding import PartitionSpec as P

EXPERTS_PER_NODE = 8
FEW_NODES = 8
COST = {"head": 100000000, "tail": 3000000000, "load": 30000000000, "join": 30000000000, "own": 100000000, "expert": 30000000000, "far0": 1, "far1": 10000000000, "fold": 1000000000, "final": 10000000000, "last": 30000000000}
PIECES = 4
HBM = pl.BlockSpec(memory_space=pltpu.HBM)
VMEM = pl.BlockSpec(memory_space=pltpu.VMEM)
SMEM = pl.BlockSpec(memory_space=pltpu.SMEM)
ROWS = (((0,), (0,)), ((), ()))
COLS = (((1,), (1,)), ((), ()))


def shift(value, axis, mask):
    size = lax.axis_size(axis)
    return lax.ppermute(value, axis, [(i, i ^ mask) for i in range(size)])


def over_nodes(pieces, known=()):
    count = len(pieces)
    known = known or [None] * count
    if count > FEW_NODES:
        moved = lax.all_to_all(jnp.stack(pieces), "node", split_axis=0, concat_axis=0, tiled=True)
        return [moved[n] for n in range(count)]
    moved = list(pieces)
    for m in range(count - 1, 0, -1):
        moved[m] = shift(pieces[m], "node", m) if known[m] is None else known[m]
    return moved


def dot(a, b, dims=(((1,), (0,)), ((), ()))):
    return lax.dot_general(a, b, dims, preferred_element_type=jnp.float32)


def bf16(value):
    return value.astype(jnp.bfloat16)


def struct(rows, cols, dtype=jnp.bfloat16):
    return jax.ShapeDtypeStruct((rows, cols), dtype)


def call(name, kernel, outs, args, specs=None, scratch=(), room=0, limit=0):
    if specs:
        args = [
            pltpu.with_memory_space_constraint(a, pltpu.HBM) if s is HBM else a
            for a, s in zip(args, specs)
        ]
    return pl.pallas_call(
        kernel,
        name="scope_" + name,
        out_shape=outs,
        in_specs=specs or [VMEM] * len(args),
        out_specs=jax.tree.map(lambda _: VMEM, outs),
        scratch_shapes=scratch,
        cost_estimate=pl.CostEstimate(flops=COST[name], bytes_accessed=0, transcendentals=0),
        compiler_params=pltpu.CompilerParams(vmem_limit_bytes=limit or (8 << 20) + room),
    )(*args)


def head_kernel(
    nodes, block, owner_ref, index_hbm, gate_hbm, tokens_hbm,
    first_ref, mix_ref, pick_ref, tokens_ref, index_ref, gate_ref, sems,
):
    copies = [
        pltpu.make_async_copy(index_hbm, index_ref, sems.at[0]),
        pltpu.make_async_copy(gate_hbm, gate_ref, sems.at[1]),
        pltpu.make_async_copy(tokens_hbm, tokens_ref, sems.at[2]),
    ]
    for copy in copies:
        copy.start()
    count, width = tokens_ref.shape
    head = first_ref.shape[0]
    row = lax.broadcasted_iota(jnp.int32, (count, count), 0)
    col = lax.broadcasted_iota(jnp.int32, (count, count), 1)
    earlier = bf16((row < col).astype(jnp.float32))
    copies[0].wait()
    copies[1].wait()
    index = index_ref[...]
    gates = gate_ref[...]
    chosen, weights = [], []
    for n in range(nodes):
        match = index == owner_ref[n]
        chosen.append(jnp.max(match.astype(jnp.float32), axis=0, keepdims=True))
        weights.append(jnp.sum(jnp.where(match, gates, 0.0), axis=0, keepdims=True))
    wanted = jnp.max(jnp.concatenate(chosen, axis=0), axis=0, keepdims=True)
    flags = jnp.concatenate(chosen + [wanted] + [jnp.zeros_like(wanted)] * (-(nodes + 1) % 8), axis=0)
    position = dot(bf16(flags), earlier)
    ahead = position[nodes : nodes + 1]
    total = jnp.sum(wanted)
    place = lax.broadcasted_iota(jnp.int32, (1, count), 1).astype(jnp.float32)
    rank = jnp.where(wanted > 0.5, ahead, total + place - ahead)
    order = bf16((rank == row.astype(jnp.float32)).astype(jnp.float32))
    slot = lax.broadcasted_iota(jnp.int32, (block, count), 0).astype(jnp.float32)
    picks, own, other = [], [], []
    for n in range(nodes):
        here = (position[n : n + 1] == slot) & (chosen[n] > 0.5)
        there = (position[n : n + 1] + block // 2 == slot) & (chosen[n] > 0.5)
        picks.append(here.astype(jnp.float32))
        own.append(jnp.where(here, weights[n], 0.0))
        other.append(jnp.where(there, weights[n], 0.0))
    own = jnp.concatenate(own, axis=0)
    other = jnp.concatenate(other, axis=0)
    own_high, other_high = bf16(own), bf16(other)
    own_low = bf16(own - own_high.astype(jnp.float32))
    other_low = bf16(other - other_high.astype(jnp.float32))
    slots = nodes * block
    mix_ref[:count] = order
    mix_ref[count : count + slots] = own_high
    mix_ref[count + slots :] = own_low
    pick_ref[...] = bf16(jnp.concatenate(picks, axis=0))
    first_ref[:, width : width + slots] = bf16(dot(order[:head], other_high, COLS))
    first_ref[:, width + slots :] = bf16(dot(order[:head], other_low, COLS))
    copies[2].wait()
    first_ref[:, :width] = bf16(dot(order[:head], tokens_ref[...]))


def tail_kernel(head, mix_ref, pick_ref, tokens_ref, near_ref, *rest):
    tokens = tokens_ref[...]
    for out in rest:
        out[...] = bf16(dot(mix_ref[head : head + out.shape[0]], tokens))
        head += out.shape[0]
    near_ref[...] = bf16(dot(pick_ref[...], tokens))


def last_kernel(start, mix_ref, tokens_ref, after_ref, out_ref):
    out_ref[...] = bf16(dot(mix_ref[start : start + out_ref.shape[0]], tokens_ref[...]))


def join_kernel(nodes, block, near_ref, first_ref, *outs):
    outs = outs[-nodes:]
    slots, width = near_ref.shape
    high = first_ref[:, width : width + slots].astype(jnp.float32)
    pick = bf16((high != 0.0).astype(jnp.float32))
    far = dot(pick, first_ref[:, :width], ROWS)
    both = near_ref[...].astype(jnp.float32) + far
    for n, out in enumerate(outs):
        out[...] = bf16(both[n * block : (n + 1) * block])


def mlp(rows, gate, up, down):
    v = dot(rows, gate[...])
    hidden = bf16(v / (1.0 + jnp.exp(-v)) * dot(rows, up[...]))
    return dot(hidden, down[...])


def load_kernel(gate_hbm, up_hbm, down_hbm, near_ref, pack_ref, sems):
    width, part = gate_hbm.shape
    copies = [(gate_hbm, 0), (up_hbm, width)]
    copies += [(down_hbm.at[:, i : i + part], 2 * width + i) for i in range(0, width, part)]
    copies = [
        pltpu.make_async_copy(
            source, pack_ref.at[place : place + source.shape[0]], sems.at[i]
        )
        for i, (source, place) in enumerate(copies)
    ]
    for copy in copies:
        copy.start()
    for copy in copies:
        copy.wait()


def expert_kernel(nodes, *refs):
    rows = [r[...] for r in refs[:nodes]]
    packs, outs = refs[nodes : nodes + 2], refs[nodes + 2 :]
    block, width = rows[0].shape
    half = block // 2
    part = packs[0].shape[1]
    rows = jnp.concatenate(rows, axis=0)
    hidden = []
    for pack in packs:
        v = dot(rows, pack[:width])
        hidden.append(bf16(v / (1.0 + jnp.exp(-v)) * dot(rows, pack[width : 2 * width])))
    for i in range(0, width, part):
        down = slice(2 * width + i, 2 * width + i + part)
        sums = dot(hidden[0], packs[0][down]) + dot(hidden[1], packs[1][down])
        start = 0
        for out in outs:
            size = out.shape[0]
            out[:, i : i + part] = bf16(sums[start : start + size])
            start += size


def blocks_of(refs, block, cols=slice(None)):
    pieces = []
    for r in refs:
        piece = r[:, cols].astype(jnp.float32)
        pieces += [piece] * (block // piece.shape[0])
    return bf16(jnp.concatenate(pieces, axis=0))


def own_kernel(
    tokens_ref, gate, up, down, after_ref, sg_hbm, su_hbm, sd_hbm, own_ref, sg, su, sd, sems,
):
    pairs = zip((sg_hbm, su_hbm, sd_hbm), (sg, su, sd))
    copies = [pltpu.make_async_copy(a, b, sems.at[i]) for i, (a, b) in enumerate(pairs)]
    for copy in copies:
        copy.start()
    rows = tokens_ref[...]
    own_ref[...] = mlp(rows, gate, up, down)
    copies[0].wait()
    v = dot(rows, sg[...])
    copies[1].wait()
    hidden = bf16(v / (1.0 + jnp.exp(-v)) * dot(rows, su[...]))
    copies[2].wait()
    own_ref[...] += dot(hidden, sd[...])


def far_kernel(groups, *refs):
    ins, mats, outs = refs[:groups], refs[groups : groups + 6], refs[groups + 6 :]
    rows = jnp.concatenate([r[:, : outs[0].shape[1]] for r in ins], axis=0)
    sums = mlp(rows, *mats[:3]) + mlp(rows, *mats[3:])
    start = 0
    for out in outs:
        out[...] = sums[start : start + out.shape[0]].astype(out.dtype)
        start += out.shape[0]


def fold_kernel(block, part_ref, first_ref, *refs):
    width = part_ref.shape[1]
    replies = blocks_of(refs[:-1], block)
    slots = replies.shape[0]
    high = first_ref[:, width : width + slots]
    low = first_ref[:, width + slots :]
    refs[-1][...] = bf16(part_ref[...] + dot(high, replies) + dot(low, replies))


def final_kernel(block, back_count, *refs):
    own_ref, mix_ref = refs[:2]
    backs, replies = refs[2 : 2 + back_count], refs[2 + back_count : -3]
    out_hbm, out_ref, sems = refs[-3:]
    width = out_ref.shape[1]
    tile = width // PIECES
    copies = []
    for i in range(PIECES):
        cols = slice(i * tile, (i + 1) * tile)
        reply = blocks_of(replies, block, cols)
        terms = jnp.concatenate([*[r[:, cols] for r in backs], reply, reply], axis=0)
        out_ref[:, cols] = bf16(own_ref[:, cols] + dot(mix_ref[...], terms, ROWS))
        copies.append(pltpu.make_async_copy(out_ref.at[:, cols], out_hbm.at[:, cols], sems.at[i]))
        copies[-1].start()
    for copy in copies:
        copy.wait()


def per_device(
    tokens, routing_gate_weight, selected_expert_index, w_gate, w_up, w_down, s_gate, s_up, s_down
):
    nodes = lax.axis_size("node")
    count, width = tokens.shape
    capacity = count // 16
    block = 2 * capacity
    slots = nodes * block
    head = min(nodes * capacity, count)
    tail = count - head

    owners = jnp.arange(nodes, dtype=jnp.int32)
    if nodes <= FEW_NODES:
        owners = owners ^ lax.axis_index("node")
    topk = selected_expert_index.shape[1]
    first, mix, pick, held = call(
        "head",
        lambda *refs: head_kernel(nodes, block, *refs),
        (
            struct(head, width + 2 * slots),
            struct(count + 2 * slots, count),
            struct(slots, count),
            struct(count, width),
        ),
        (owners * EXPERTS_PER_NODE, selected_expert_index.T, routing_gate_weight.T, tokens),
        specs=[SMEM, HBM, HBM, HBM],
        scratch=[
            pltpu.VMEM((topk, count), jnp.int32),
            pltpu.VMEM((topk, count), jnp.float32),
            pltpu.SemaphoreType.DMA((3,)),
        ],
        limit=16 << 20,
    )
    far_first = shift(first, "local", 2)
    cut = tail * 4 // 6 // 16 * 16
    near, *rest = call(
        "tail",
        lambda *refs: tail_kernel(head, *refs),
        [struct(slots, width)] + [struct(cut, width)] * (cut > 0),
        (mix, pick, held),
        room=4 * (slots + count) * width,
    )
    rest_far = [shift(r, "local", 2) for r in rest]
    shared_mats = (s_gate, s_up, s_down)
    shared_far = [shift(w, "local", 1) for w in shared_mats]
    sent = call(
        "join",
        lambda *refs: join_kernel(nodes, block, *refs),
        [struct(block, width)] * nodes,
        (near, far_first, *[]),
        room=8 * slots * width,
    )
    part = w_gate.shape[2]
    pack = call(
        "load",
        load_kernel,
        struct(3 * width, part),
        (w_gate[0], w_up[0], w_down[0], first),
        specs=[HBM] * 3 + [VMEM],
        scratch=[pltpu.SemaphoreType.DMA((2 + width // part,))],
        limit=16 << 20,
    )
    far_pack = shift(pack, "local", 1)
    arrived = over_nodes(sent)
    if tail > cut:
        last = call(
            "last",
            lambda *refs: last_kernel(head + cut, *refs),
            struct(tail - cut, width),
            (mix, held, sent[0]),
            room=4 * count * width,
        )
        rest_far.append(shift(last, "local", 2))
    own, *mats = call(
        "own",
        own_kernel,
        [
            struct(count, width, jnp.float32),
            *[struct(*w.shape) for w in shared_mats],
        ],
        (held, *shared_far, near, *shared_mats),
        specs=[VMEM] * 5 + [HBM] * 3,
        scratch=[pltpu.SemaphoreType.DMA((3,))],
        limit=16 << 20,
    )
    whole = [n == 1 and nodes <= FEW_NODES for n in range(nodes)]
    replied = call(
        "expert",
        lambda *refs: expert_kernel(nodes, *refs),
        [
            struct(rows, width)
            for n in range(nodes)
            for rows in ([block] if whole[n] else [capacity] * 2)
        ],
        (*arrived, pack, far_pack),
        room=20 * slots * width + (4 << 20),
    )
    split = iter(replied)
    pairs = [[next(split)] if w else [next(split), next(split)] for w in whole]
    far_replies = over_nodes([p[-1] for p in pairs])
    replies = over_nodes([p[0] for p in pairs], [f if w else None for f, w in zip(far_replies, whole)])

    sums, late = [], []
    for i, rows in enumerate(([far_first] + rest_far[:1], rest_far[1:])):
        if rows:
            sums += call(
                "far" + str(i),
                lambda *refs, n=len(rows): far_kernel(n, *refs),
                [
                    struct(r.shape[0], width, jnp.float32 if r is far_first else jnp.bfloat16)
                    for r in rows
                ],
                (*rows, *shared_far, *mats),
                room=12 * count * width,
            )
    late = [shift(r, "local", 2) for r in sums[1:]]
    folded = call(
        "fold",
        lambda *refs: fold_kernel(block, *refs),
        struct(head, width),
        (sums[0], far_first, *far_replies),
        room=8 * slots * width,
    )
    backs = [shift(folded, "local", 2)] + late
    return pl.pallas_call(
        lambda *refs: final_kernel(block, len(backs), *refs),
        name="scope_final",
        out_shape=struct(count, width),
        in_specs=[VMEM] * (2 + len(backs) + nodes),
        out_specs=HBM,
        scratch_shapes=[
            pltpu.VMEM((count, width), jnp.bfloat16),
            pltpu.SemaphoreType.DMA((PIECES,)),
        ],
        cost_estimate=pl.CostEstimate(flops=COST["final"], bytes_accessed=0, transcendentals=0),
        compiler_params=pltpu.CompilerParams(vmem_limit_bytes=(8 << 20) + 8 * slots * width),
    )(own, mix, *backs, *replies)


def solution(mesh):
    in_specs = (
        P(("groups", "node", "local"), None),
        P(("groups", "node", "local"), None),
        P(("groups", "node", "local"), None),
        P("node", None, "local"),
        P("node", None, "local"),
        P("node", "local", None),
        P(None, "local"),
        P(None, "local"),
        P("local", None),
    )
    out_specs = P(("groups", "node", "local"), None)
    return jax.shard_map(
        per_device, mesh=mesh, in_specs=in_specs, out_specs=out_specs, check_vma=False
    )
```

```python
import jax
import jax.numpy as jnp
from jax import lax
from jax.experimental import pallas as pl
from jax.experimental.pallas import tpu as pltpu
from jax.sharding import PartitionSpec as P

EXPERTS_PER_NODE = 8
FEW_NODES = 8
COST = {"head": 100000000, "tail": 3000000000, "load": 30000000000, "join": 30000000000, "own": 100000000, "expert": 30000000000, "far0": 1, "far1": 10000000000, "fold": 1000000000, "final": 10000000000, "last": 30000000000}
PIECES = 4
HBM = pl.BlockSpec(memory_space=pltpu.HBM)
VMEM = pl.BlockSpec(memory_space=pltpu.VMEM)
SMEM = pl.BlockSpec(memory_space=pltpu.SMEM)
ROWS = (((0,), (0,)), ((), ()))
COLS = (((1,), (1,)), ((), ()))


def shift(value, axis, mask):
    size = lax.axis_size(axis)
    return lax.ppermute(value, axis, [(i, i ^ mask) for i in range(size)])


def over_nodes(pieces, known=()):
    count = len(pieces)
    known = known or [None] * count
    if count > FEW_NODES:
        moved = lax.all_to_all(jnp.stack(pieces), "node", split_axis=0, concat_axis=0, tiled=True)
        return [moved[n] for n in range(count)]
    moved = list(pieces)
    for m in range(count - 1, 0, -1):
        moved[m] = shift(pieces[m], "node", m) if known[m] is None else known[m]
    return moved


def dot(a, b, dims=(((1,), (0,)), ((), ()))):
    return lax.dot_general(a, b, dims, preferred_element_type=jnp.float32)


def bf16(value):
    return value.astype(jnp.bfloat16)


def struct(rows, cols, dtype=jnp.bfloat16):
    return jax.ShapeDtypeStruct((rows, cols), dtype)


def call(name, kernel, outs, args, specs=None, scratch=(), room=0, limit=0):
    if specs:
        args = [
            pltpu.with_memory_space_constraint(a, pltpu.HBM) if s is HBM else a
            for a, s in zip(args, specs)
        ]
    return pl.pallas_call(
        kernel,
        name="scope_" + name,
        out_shape=outs,
        in_specs=specs or [VMEM] * len(args),
        out_specs=jax.tree.map(lambda _: VMEM, outs),
        scratch_shapes=scratch,
        cost_estimate=pl.CostEstimate(flops=COST[name], bytes_accessed=0, transcendentals=0),
        compiler_params=pltpu.CompilerParams(vmem_limit_bytes=limit or (8 << 20) + room),
    )(*args)


def head_kernel(
    nodes, block, owner_ref, index_hbm, gate_hbm, tokens_hbm,
    first_ref, mix_ref, pick_ref, tokens_ref, index_ref, gate_ref, sems,
):
    copies = [
        pltpu.make_async_copy(index_hbm, index_ref, sems.at[0]),
        pltpu.make_async_copy(gate_hbm, gate_ref, sems.at[1]),
        pltpu.make_async_copy(tokens_hbm, tokens_ref, sems.at[2]),
    ]
    for copy in copies:
        copy.start()
    count, width = tokens_ref.shape
    head = first_ref.shape[0]
    row = lax.broadcasted_iota(jnp.int32, (count, count), 0)
    col = lax.broadcasted_iota(jnp.int32, (count, count), 1)
    earlier = bf16((row < col).astype(jnp.float32))
    copies[0].wait()
    copies[1].wait()
    index = index_ref[...]
    gates = gate_ref[...]
    chosen, weights = [], []
    for n in range(nodes):
        match = index == owner_ref[n]
        chosen.append(jnp.max(match.astype(jnp.float32), axis=0, keepdims=True))
        weights.append(jnp.sum(jnp.where(match, gates, 0.0), axis=0, keepdims=True))
    wanted = jnp.max(jnp.concatenate(chosen, axis=0), axis=0, keepdims=True)
    flags = jnp.concatenate(chosen + [wanted] + [jnp.zeros_like(wanted)] * (-(nodes + 1) % 8), axis=0)
    position = dot(bf16(flags), earlier)
    ahead = position[nodes : nodes + 1]
    total = jnp.sum(wanted)
    place = lax.broadcasted_iota(jnp.int32, (1, count), 1).astype(jnp.float32)
    rank = jnp.where(wanted > 0.5, ahead, total + place - ahead)
    order = bf16((rank == row.astype(jnp.float32)).astype(jnp.float32))
    slot = lax.broadcasted_iota(jnp.int32, (block, count), 0).astype(jnp.float32)
    picks, own, other = [], [], []
    for n in range(nodes):
        here = (position[n : n + 1] == slot) & (chosen[n] > 0.5)
        there = (position[n : n + 1] + block // 2 == slot) & (chosen[n] > 0.5)
        picks.append(here.astype(jnp.float32))
        own.append(jnp.where(here, weights[n], 0.0))
        other.append(jnp.where(there, weights[n], 0.0))
    own = jnp.concatenate(own, axis=0)
    other = jnp.concatenate(other, axis=0)
    own_high, other_high = bf16(own), bf16(other)
    own_low = bf16(own - own_high.astype(jnp.float32))
    other_low = bf16(other - other_high.astype(jnp.float32))
    slots = nodes * block
    mix_ref[:count] = order
    mix_ref[count : count + slots] = own_high
    mix_ref[count + slots :] = own_low
    pick_ref[...] = bf16(jnp.concatenate(picks, axis=0))
    first_ref[:, width : width + slots] = bf16(dot(order[:head], other_high, COLS))
    first_ref[:, width + slots :] = bf16(dot(order[:head], other_low, COLS))
    copies[2].wait()
    first_ref[:, :width] = bf16(dot(order[:head], tokens_ref[...]))


def tail_kernel(head, mix_ref, pick_ref, tokens_ref, near_ref, *rest):
    tokens = tokens_ref[...]
    for out in rest:
        out[...] = bf16(dot(mix_ref[head : head + out.shape[0]], tokens))
        head += out.shape[0]
    near_ref[...] = bf16(dot(pick_ref[...], tokens))


def last_kernel(start, mix_ref, tokens_ref, after_ref, out_ref):
    out_ref[...] = bf16(dot(mix_ref[start : start + out_ref.shape[0]], tokens_ref[...]))


def join_kernel(nodes, block, near_ref, first_ref, *outs):
    outs = outs[-nodes:]
    slots, width = near_ref.shape
    high = first_ref[:, width : width + slots].astype(jnp.float32)
    pick = bf16((high != 0.0).astype(jnp.float32))
    far = dot(pick, first_ref[:, :width], ROWS)
    both = near_ref[...].astype(jnp.float32) + far
    for n, out in enumerate(outs):
        out[...] = bf16(both[n * block : (n + 1) * block])


def mlp(rows, gate, up, down):
    v = dot(rows, gate[...])
    hidden = bf16(v / (1.0 + jnp.exp(-v)) * dot(rows, up[...]))
    return dot(hidden, down[...])


def load_kernel(gate_hbm, up_hbm, down_hbm, sg_hbm, near_ref, pack_ref, sg, sems):
    width, part = gate_hbm.shape
    copies = [(gate_hbm, 0), (up_hbm, width)]
    copies += [(down_hbm.at[:, i : i + part], 2 * width + i) for i in range(0, width, part)]
    copies = [
        pltpu.make_async_copy(
            source, pack_ref.at[place : place + source.shape[0]], sems.at[i]
        )
        for i, (source, place) in enumerate(copies)
    ]
    copies.append(pltpu.make_async_copy(sg_hbm, sg, sems.at[len(copies)]))
    for copy in copies:
        copy.start()
    for copy in copies:
        copy.wait()


def expert_kernel(nodes, *refs):
    rows = [r[...] for r in refs[:nodes]]
    packs, outs = refs[nodes : nodes + 2], refs[nodes + 2 :]
    block, width = rows[0].shape
    half = block // 2
    part = packs[0].shape[1]
    rows = jnp.concatenate(rows, axis=0)
    hidden = []
    for pack in packs:
        v = dot(rows, pack[:width])
        hidden.append(bf16(v / (1.0 + jnp.exp(-v)) * dot(rows, pack[width : 2 * width])))
    for i in range(0, width, part):
        down = slice(2 * width + i, 2 * width + i + part)
        sums = dot(hidden[0], packs[0][down]) + dot(hidden[1], packs[1][down])
        start = 0
        for out in outs:
            size = out.shape[0]
            out[:, i : i + part] = bf16(sums[start : start + size])
            start += size


def blocks_of(refs, block, cols=slice(None)):
    pieces = []
    for r in refs:
        piece = r[:, cols].astype(jnp.float32)
        pieces += [piece] * (block // piece.shape[0])
    return bf16(jnp.concatenate(pieces, axis=0))


def own_kernel(
    tokens_ref, gate, up, down, after_ref, sg, su_hbm, sd_hbm, own_ref, su, sd, sems
):
    copies = [
        pltpu.make_async_copy(su_hbm, su, sems.at[0]),
        pltpu.make_async_copy(sd_hbm, sd, sems.at[1]),
    ]
    for copy in copies:
        copy.start()
    rows = tokens_ref[...]
    v = dot(rows, gate[...])
    hidden = bf16(v / (1.0 + jnp.exp(-v)) * dot(rows, up[...]))
    v = dot(rows, sg[...])
    copies[0].wait()
    own_hidden = bf16(v / (1.0 + jnp.exp(-v)) * dot(rows, su[...]))
    copies[1].wait()
    own_ref[...] = dot(hidden, down[...]) + dot(own_hidden, sd[...])


def far_kernel(groups, *refs):
    ins, mats, outs = refs[:groups], refs[groups : groups + 6], refs[groups + 6 :]
    rows = jnp.concatenate([r[:, : outs[0].shape[1]] for r in ins], axis=0)
    sums = mlp(rows, *mats[:3]) + mlp(rows, *mats[3:])
    start = 0
    for out in outs:
        out[...] = sums[start : start + out.shape[0]].astype(out.dtype)
        start += out.shape[0]


def fold_kernel(block, part_ref, first_ref, *refs):
    width = part_ref.shape[1]
    replies = blocks_of(refs[:-1], block)
    slots = replies.shape[0]
    high = first_ref[:, width : width + slots]
    low = first_ref[:, width + slots :]
    refs[-1][...] = bf16(part_ref[...] + dot(high, replies) + dot(low, replies))


def final_kernel(block, back_count, *refs):
    own_ref, mix_ref = refs[:2]
    backs, replies = refs[2 : 2 + back_count], refs[2 + back_count : -3]
    out_hbm, out_ref, sems = refs[-3:]
    width = out_ref.shape[1]
    tile = width // PIECES
    copies = []
    for i in range(PIECES):
        cols = slice(i * tile, (i + 1) * tile)
        reply = blocks_of(replies, block, cols)
        terms = jnp.concatenate([*[r[:, cols] for r in backs], reply, reply], axis=0)
        out_ref[:, cols] = bf16(own_ref[:, cols] + dot(mix_ref[...], terms, ROWS))
        copies.append(pltpu.make_async_copy(out_ref.at[:, cols], out_hbm.at[:, cols], sems.at[i]))
        copies[-1].start()
    for copy in copies:
        copy.wait()


def per_device(
    tokens, routing_gate_weight, selected_expert_index, w_gate, w_up, w_down, s_gate, s_up, s_down
):
    nodes = lax.axis_size("node")
    count, width = tokens.shape
    capacity = count // 16
    block = 2 * capacity
    slots = nodes * block
    head = min(nodes * capacity, count)
    tail = count - head

    owners = jnp.arange(nodes, dtype=jnp.int32)
    if nodes <= FEW_NODES:
        owners = owners ^ lax.axis_index("node")
    topk = selected_expert_index.shape[1]
    first, mix, pick, held = call(
        "head",
        lambda *refs: head_kernel(nodes, block, *refs),
        (
            struct(head, width + 2 * slots),
            struct(count + 2 * slots, count),
            struct(slots, count),
            struct(count, width),
        ),
        (owners * EXPERTS_PER_NODE, selected_expert_index.T, routing_gate_weight.T, tokens),
        specs=[SMEM, HBM, HBM, HBM],
        scratch=[
            pltpu.VMEM((topk, count), jnp.int32),
            pltpu.VMEM((topk, count), jnp.float32),
            pltpu.SemaphoreType.DMA((3,)),
        ],
        limit=16 << 20,
    )
    far_first = shift(first, "local", 2)
    cut = tail * 4 // 6 // 16 * 16
    near, *rest = call(
        "tail",
        lambda *refs: tail_kernel(head, *refs),
        [struct(slots, width)] + [struct(cut, width)] * (cut > 0),
        (mix, pick, held),
        room=4 * (slots + count) * width,
    )
    rest_far = [shift(r, "local", 2) for r in rest]
    shared_mats = (s_gate, s_up, s_down)
    shared_far = [shift(w, "local", 1) for w in shared_mats]
    sent = call(
        "join",
        lambda *refs: join_kernel(nodes, block, *refs),
        [struct(block, width)] * nodes,
        (near, far_first, *[]),
        room=8 * slots * width,
    )
    part = w_gate.shape[2]
    pack, own_gate = call(
        "load",
        load_kernel,
        [struct(3 * width, part), struct(*s_gate.shape)],
        (w_gate[0], w_up[0], w_down[0], s_gate, first),
        specs=[HBM] * 4 + [VMEM],
        scratch=[pltpu.SemaphoreType.DMA((3 + width // part,))],
        limit=16 << 20,
    )
    far_pack = shift(pack, "local", 1)
    arrived = over_nodes(sent)
    if tail > cut:
        last = call(
            "last",
            lambda *refs: last_kernel(head + cut, *refs),
            struct(tail - cut, width),
            (mix, held, sent[0]),
            room=4 * count * width,
        )
        rest_far.append(shift(last, "local", 2))
    own, *mats = call(
        "own",
        own_kernel,
        [struct(count, width, jnp.float32)] + [struct(*w.shape) for w in shared_mats[1:]],
        (held, *shared_far, near, own_gate, *shared_mats[1:]),
        specs=[VMEM] * 6 + [HBM] * 2,
        scratch=[pltpu.SemaphoreType.DMA((2,))],
        limit=16 << 20,
    )
    mats = [own_gate, *mats]
    whole = [n == 1 and nodes <= FEW_NODES for n in range(nodes)]
    replied = call(
        "expert",
        lambda *refs: expert_kernel(nodes, *refs),
        [
            struct(rows, width)
            for n in range(nodes)
            for rows in ([block] if whole[n] else [capacity] * 2)
        ],
        (*arrived, pack, far_pack),
        room=20 * slots * width + (4 << 20),
    )
    split = iter(replied)
    pairs = [[next(split)] if w else [next(split), next(split)] for w in whole]
    far_replies = over_nodes([p[-1] for p in pairs])
    replies = over_nodes([p[0] for p in pairs], [f if w else None for f, w in zip(far_replies, whole)])

    sums, late = [], []
    for i, rows in enumerate(([far_first] + rest_far[:1], rest_far[1:])):
        if rows:
            sums += call(
                "far" + str(i),
                lambda *refs, n=len(rows): far_kernel(n, *refs),
                [
                    struct(r.shape[0], width, jnp.float32 if r is far_first else jnp.bfloat16)
                    for r in rows
                ],
                (*rows, *shared_far, *mats),
                room=12 * count * width,
            )
    late = [shift(r, "local", 2) for r in sums[1:]]
    folded = call(
        "fold",
        lambda *refs: fold_kernel(block, *refs),
        struct(head, width),
        (sums[0], far_first, *far_replies),
        room=8 * slots * width,
    )
    backs = [shift(folded, "local", 2)] + late
    return pl.pallas_call(
        lambda *refs: final_kernel(block, len(backs), *refs),
        name="scope_final",
        out_shape=struct(count, width),
        in_specs=[VMEM] * (2 + len(backs) + nodes),
        out_specs=HBM,
        scratch_shapes=[
            pltpu.VMEM((count, width), jnp.bfloat16),
            pltpu.SemaphoreType.DMA((PIECES,)),
        ],
        cost_estimate=pl.CostEstimate(flops=COST["final"], bytes_accessed=0, transcendentals=0),
        compiler_params=pltpu.CompilerParams(vmem_limit_bytes=(8 << 20) + 8 * slots * width),
    )(own, mix, *backs, *replies)


def solution(mesh):
    in_specs = (
        P(("groups", "node", "local"), None),
        P(("groups", "node", "local"), None),
        P(("groups", "node", "local"), None),
        P("node", None, "local"),
        P("node", None, "local"),
        P("node", "local", None),
        P(None, "local"),
        P(None, "local"),
        P("local", None),
    )
    out_specs = P(("groups", "node", "local"), None)
    return jax.shard_map(
        per_device, mesh=mesh, in_specs=in_specs, out_specs=out_specs, check_vma=False
    )
```

```python
import jax
import jax.numpy as jnp
from jax import lax
from jax.experimental import pallas as pl
from jax.experimental.pallas import tpu as pltpu
from jax.sharding import PartitionSpec as P

EXPERTS_PER_NODE = 8
FEW_NODES = 8
COST = {"head": 100000000, "tail": 3000000000, "load": 30000000000, "join": 30000000000, "own": 100000000, "expert": 30000000000, "far0": 1, "far1": 10000000000, "fold": 1000000000, "final": 10000000000, "last": 30000000000}
PIECES = 4
HBM = pl.BlockSpec(memory_space=pltpu.HBM)
VMEM = pl.BlockSpec(memory_space=pltpu.VMEM)
SMEM = pl.BlockSpec(memory_space=pltpu.SMEM)
ROWS = (((0,), (0,)), ((), ()))
COLS = (((1,), (1,)), ((), ()))


def shift(value, axis, mask):
    size = lax.axis_size(axis)
    return lax.ppermute(value, axis, [(i, i ^ mask) for i in range(size)])


def over_nodes(pieces, known=()):
    count = len(pieces)
    known = known or [None] * count
    if count > FEW_NODES:
        moved = lax.all_to_all(jnp.stack(pieces), "node", split_axis=0, concat_axis=0, tiled=True)
        return [moved[n] for n in range(count)]
    moved = list(pieces)
    for m in range(count - 1, 0, -1):
        moved[m] = shift(pieces[m], "node", m) if known[m] is None else known[m]
    return moved


def dot(a, b, dims=(((1,), (0,)), ((), ()))):
    return lax.dot_general(a, b, dims, preferred_element_type=jnp.float32)


def bf16(value):
    return value.astype(jnp.bfloat16)


def struct(rows, cols, dtype=jnp.bfloat16):
    return jax.ShapeDtypeStruct((rows, cols), dtype)


def call(name, kernel, outs, args, specs=None, scratch=(), room=0, limit=0):
    if specs:
        args = [
            pltpu.with_memory_space_constraint(a, pltpu.HBM) if s is HBM else a
            for a, s in zip(args, specs)
        ]
    return pl.pallas_call(
        kernel,
        name="scope_" + name,
        out_shape=outs,
        in_specs=specs or [VMEM] * len(args),
        out_specs=jax.tree.map(lambda _: VMEM, outs),
        scratch_shapes=scratch,
        cost_estimate=pl.CostEstimate(flops=COST[name], bytes_accessed=0, transcendentals=0),
        compiler_params=pltpu.CompilerParams(vmem_limit_bytes=limit or (8 << 20) + room),
    )(*args)


def head_kernel(
    nodes, block, owner_ref, index_hbm, gate_hbm, tokens_hbm,
    first_ref, mix_ref, pick_ref, tokens_ref, index_ref, gate_ref, sems,
):
    copies = [
        pltpu.make_async_copy(index_hbm, index_ref, sems.at[0]),
        pltpu.make_async_copy(gate_hbm, gate_ref, sems.at[1]),
        pltpu.make_async_copy(tokens_hbm, tokens_ref, sems.at[2]),
    ]
    for copy in copies:
        copy.start()
    count, width = tokens_ref.shape
    head = first_ref.shape[0]
    row = lax.broadcasted_iota(jnp.int32, (count, count), 0)
    col = lax.broadcasted_iota(jnp.int32, (count, count), 1)
    earlier = bf16((row < col).astype(jnp.float32))
    copies[0].wait()
    copies[1].wait()
    index = index_ref[...]
    gates = gate_ref[...]
    chosen, weights = [], []
    for n in range(nodes):
        match = index == owner_ref[n]
        chosen.append(jnp.max(match.astype(jnp.float32), axis=0, keepdims=True))
        weights.append(jnp.sum(jnp.where(match, gates, 0.0), axis=0, keepdims=True))
    wanted = jnp.max(jnp.concatenate(chosen, axis=0), axis=0, keepdims=True)
    flags = jnp.concatenate(chosen + [wanted] + [jnp.zeros_like(wanted)] * (-(nodes + 1) % 8), axis=0)
    position = dot(bf16(flags), earlier)
    ahead = position[nodes : nodes + 1]
    total = jnp.sum(wanted)
    place = lax.broadcasted_iota(jnp.int32, (1, count), 1).astype(jnp.float32)
    rank = jnp.where(wanted > 0.5, ahead, total + place - ahead)
    order = bf16((rank == row.astype(jnp.float32)).astype(jnp.float32))
    slot = lax.broadcasted_iota(jnp.int32, (block, count), 0).astype(jnp.float32)
    picks, own, other = [], [], []
    for n in range(nodes):
        here = (position[n : n + 1] == slot) & (chosen[n] > 0.5)
        there = (position[n : n + 1] + block // 2 == slot) & (chosen[n] > 0.5)
        picks.append(here.astype(jnp.float32))
        own.append(jnp.where(here, weights[n], 0.0))
        other.append(jnp.where(there, weights[n], 0.0))
    own = jnp.concatenate(own, axis=0)
    other = jnp.concatenate(other, axis=0)
    own_high, other_high = bf16(own), bf16(other)
    own_low = bf16(own - own_high.astype(jnp.float32))
    other_low = bf16(other - other_high.astype(jnp.float32))
    slots = nodes * block
    mix_ref[:count] = order
    mix_ref[count : count + slots] = own_high
    mix_ref[count + slots :] = own_low
    pick_ref[...] = bf16(jnp.concatenate(picks, axis=0))
    first_ref[:, width : width + slots] = bf16(dot(order[:head], other_high, COLS))
    first_ref[:, width + slots :] = bf16(dot(order[:head], other_low, COLS))
    copies[2].wait()
    first_ref[:, :width] = bf16(dot(order[:head], tokens_ref[...]))


def tail_kernel(head, mix_ref, pick_ref, tokens_ref, near_ref, *rest):
    tokens = tokens_ref[...]
    for out in rest:
        out[...] = bf16(dot(mix_ref[head : head + out.shape[0]], tokens))
        head += out.shape[0]
    near_ref[...] = bf16(dot(pick_ref[...], tokens))


def last_kernel(start, mix_ref, tokens_ref, after_ref, out_ref):
    out_ref[...] = bf16(dot(mix_ref[start : start + out_ref.shape[0]], tokens_ref[...]))


def join_kernel(nodes, block, near_ref, first_ref, *outs):
    outs = outs[-nodes:]
    slots, width = near_ref.shape
    high = first_ref[:, width : width + slots].astype(jnp.float32)
    pick = bf16((high != 0.0).astype(jnp.float32))
    far = dot(pick, first_ref[:, :width], ROWS)
    both = near_ref[...].astype(jnp.float32) + far
    for n, out in enumerate(outs):
        out[...] = bf16(both[n * block : (n + 1) * block])


def mlp(rows, gate, up, down):
    v = dot(rows, gate[...])
    hidden = bf16(v / (1.0 + jnp.exp(-v)) * dot(rows, up[...]))
    return dot(hidden, down[...])


def load_kernel(gate_hbm, up_hbm, down_hbm, sg_hbm, near_ref, pack_ref, sg, sems):
    width, part = gate_hbm.shape
    copies = [(gate_hbm, 0), (up_hbm, width)]
    copies += [(down_hbm.at[:, i : i + part], 2 * width + i) for i in range(0, width, part)]
    copies = [
        pltpu.make_async_copy(
            source, pack_ref.at[place : place + source.shape[0]], sems.at[i]
        )
        for i, (source, place) in enumerate(copies)
    ]
    copies.append(pltpu.make_async_copy(sg_hbm, sg, sems.at[len(copies)]))
    for copy in copies:
        copy.start()
    for copy in copies:
        copy.wait()


def expert_kernel(nodes, *refs):
    rows = [r[...] for r in refs[:nodes]]
    packs, outs = refs[nodes : nodes + 2], refs[nodes + 2 :]
    block, width = rows[0].shape
    half = block // 2
    part = packs[0].shape[1]
    rows = jnp.concatenate(rows, axis=0)
    hidden = []
    for pack in packs:
        v = dot(rows, pack[:width])
        hidden.append(bf16(v / (1.0 + jnp.exp(-v)) * dot(rows, pack[width : 2 * width])))
    for i in range(0, width, part):
        down = slice(2 * width + i, 2 * width + i + part)
        sums = dot(hidden[0], packs[0][down]) + dot(hidden[1], packs[1][down])
        start = 0
        for out in outs:
            size = out.shape[0]
            out[:, i : i + part] = bf16(sums[start : start + size])
            start += size


def blocks_of(refs, block, cols=slice(None)):
    pieces = []
    for r in refs:
        piece = r[:, cols].astype(jnp.float32)
        pieces += [piece] * (block // piece.shape[0])
    return bf16(jnp.concatenate(pieces, axis=0))


def own_kernel(
    tokens_ref, gate, up, down, after_ref, sg, su_hbm, sd_hbm, own_ref, su, sd, sems
):
    copies = [
        pltpu.make_async_copy(su_hbm, su, sems.at[0]),
        pltpu.make_async_copy(sd_hbm, sd, sems.at[1]),
    ]
    for copy in copies:
        copy.start()
    rows = tokens_ref[...]
    own_ref[...] = mlp(rows, gate, up, down)
    v = dot(rows, sg[...])
    copies[0].wait()
    hidden = bf16(v / (1.0 + jnp.exp(-v)) * dot(rows, su[...]))
    copies[1].wait()
    own_ref[...] += dot(hidden, sd[...])


def far_kernel(groups, *refs):
    ins, mats, outs = refs[:groups], refs[groups : groups + 6], refs[groups + 6 :]
    rows = jnp.concatenate([r[:, : outs[0].shape[1]] for r in ins], axis=0)
    sums = mlp(rows, *mats[:3]) + mlp(rows, *mats[3:])
    start = 0
    for out in outs:
        out[...] = sums[start : start + out.shape[0]].astype(out.dtype)
        start += out.shape[0]


def fold_kernel(block, part_ref, first_ref, *refs):
    width = part_ref.shape[1]
    replies = blocks_of(refs[:-1], block)
    slots = replies.shape[0]
    high = first_ref[:, width : width + slots]
    low = first_ref[:, width + slots :]
    refs[-1][...] = bf16(part_ref[...] + dot(high, replies) + dot(low, replies))


def final_kernel(block, back_count, *refs):
    own_ref, mix_ref = refs[:2]
    backs, replies = refs[2 : 2 + back_count], refs[2 + back_count : -3]
    out_hbm, out_ref, sems = refs[-3:]
    width = out_ref.shape[1]
    tile = width // PIECES
    copies = []
    for i in range(PIECES):
        cols = slice(i * tile, (i + 1) * tile)
        reply = blocks_of(replies, block, cols)
        terms = jnp.concatenate([*[r[:, cols] for r in backs], reply, reply], axis=0)
        out_ref[:, cols] = bf16(own_ref[:, cols] + dot(mix_ref[...], terms, ROWS))
        copies.append(pltpu.make_async_copy(out_ref.at[:, cols], out_hbm.at[:, cols], sems.at[i]))
        copies[-1].start()
    for copy in copies:
        copy.wait()


def per_device(
    tokens, routing_gate_weight, selected_expert_index, w_gate, w_up, w_down, s_gate, s_up, s_down
):
    nodes = lax.axis_size("node")
    count, width = tokens.shape
    capacity = count // 16
    block = 2 * capacity
    slots = nodes * block
    head = min(nodes * capacity, count)
    tail = count - head

    owners = jnp.arange(nodes, dtype=jnp.int32)
    if nodes <= FEW_NODES:
        owners = owners ^ lax.axis_index("node")
    topk = selected_expert_index.shape[1]
    first, mix, pick, held = call(
        "head",
        lambda *refs: head_kernel(nodes, block, *refs),
        (
            struct(head, width + 2 * slots),
            struct(count + 2 * slots, count),
            struct(slots, count),
            struct(count, width),
        ),
        (owners * EXPERTS_PER_NODE, selected_expert_index.T, routing_gate_weight.T, tokens),
        specs=[SMEM, HBM, HBM, HBM],
        scratch=[
            pltpu.VMEM((topk, count), jnp.int32),
            pltpu.VMEM((topk, count), jnp.float32),
            pltpu.SemaphoreType.DMA((3,)),
        ],
        limit=16 << 20,
    )
    far_first = shift(first, "local", 2)
    cut = tail * 4 // 6 // 16 * 16
    near, *rest = call(
        "tail",
        lambda *refs: tail_kernel(head, *refs),
        [struct(slots, width)] + [struct(cut, width)] * (cut > 0),
        (mix, pick, held),
        room=4 * (slots + count) * width,
    )
    rest_far = [shift(r, "local", 2) for r in rest]
    shared_mats = (s_gate, s_up, s_down)
    shared_far = [shift(w, "local", 1) for w in shared_mats]
    sent = call(
        "join",
        lambda *refs: join_kernel(nodes, block, *refs),
        [struct(block, width)] * nodes,
        (near, far_first, *[]),
        room=8 * slots * width,
    )
    part = w_gate.shape[2]
    pack, own_gate = call(
        "load",
        load_kernel,
        [struct(3 * width, part), struct(*s_gate.shape)],
        (w_gate[0], w_up[0], w_down[0], s_gate, first),
        specs=[HBM] * 4 + [VMEM],
        scratch=[pltpu.SemaphoreType.DMA((3 + width // part,))],
        limit=16 << 20,
    )
    far_pack = shift(pack, "local", 1)
    arrived = over_nodes(sent)
    if tail > cut:
        last = call(
            "last",
            lambda *refs: last_kernel(head + cut, *refs),
            struct(tail - cut, width),
            (mix, held, sent[0]),
            room=4 * count * width,
        )
        rest_far.append(shift(last, "local", 2))
    own, *mats = call(
        "own",
        own_kernel,
        [struct(count, width, jnp.float32)] + [struct(*w.shape) for w in shared_mats[1:]],
        (held, *shared_far, near, own_gate, *shared_mats[1:]),
        specs=[VMEM] * 6 + [HBM] * 2,
        scratch=[pltpu.SemaphoreType.DMA((2,))],
        limit=16 << 20,
    )
    mats = [own_gate, *mats]
    whole = [n == 1 and nodes <= FEW_NODES for n in range(nodes)]
    replied = call(
        "expert",
        lambda *refs: expert_kernel(nodes, *refs),
        [
            struct(rows, width)
            for n in range(nodes)
            for rows in ([block] if whole[n] else [capacity] * 2)
        ],
        (*arrived, pack, far_pack),
        room=20 * slots * width + (4 << 20),
    )
    split = iter(replied)
    pairs = [[next(split)] if w else [next(split), next(split)] for w in whole]
    far_replies = over_nodes([p[-1] for p in pairs])
    replies = over_nodes([p[0] for p in pairs], [f if w else None for f, w in zip(far_replies, whole)])

    sums, late = [], []
    for i, rows in enumerate(([far_first] + rest_far[:1], rest_far[1:])):
        if rows:
            sums += call(
                "far" + str(i),
                lambda *refs, n=len(rows): far_kernel(n, *refs),
                [
                    struct(r.shape[0], width, jnp.float32 if r is far_first else jnp.bfloat16)
                    for r in rows
                ],
                (*rows, *shared_far, *mats),
                room=12 * count * width,
            )
    late = [shift(r, "local", 2) for r in sums[1:]]
    folded = call(
        "fold",
        lambda *refs: fold_kernel(block, *refs),
        struct(head, width),
        (sums[0], far_first, *far_replies),
        room=8 * slots * width,
    )
    backs = [shift(folded, "local", 2)] + late
    return pl.pallas_call(
        lambda *refs: final_kernel(block, len(backs), *refs),
        name="scope_final",
        out_shape=struct(count, width),
        in_specs=[VMEM] * (2 + len(backs) + nodes),
        out_specs=HBM,
        scratch_shapes=[
            pltpu.VMEM((count, width), jnp.bfloat16),
            pltpu.SemaphoreType.DMA((PIECES,)),
        ],
        cost_estimate=pl.CostEstimate(flops=COST["final"], bytes_accessed=0, transcendentals=0),
        compiler_params=pltpu.CompilerParams(vmem_limit_bytes=(8 << 20) + 8 * slots * width),
    )(own, mix, *backs, *replies)


def solution(mesh):
    in_specs = (
        P(("groups", "node", "local"), None),
        P(("groups", "node", "local"), None),
        P(("groups", "node", "local"), None),
        P("node", None, "local"),
        P("node", None, "local"),
        P("node", "local", None),
        P(None, "local"),
        P(None, "local"),
        P("local", None),
    )
    out_specs = P(("groups", "node", "local"), None)
    return jax.shard_map(
        per_device, mesh=mesh, in_specs=in_specs, out_specs=out_specs, check_vma=False
    )
```

```python
import jax
import jax.numpy as jnp
from jax import lax
from jax.experimental import pallas as pl
from jax.experimental.pallas import tpu as pltpu
from jax.sharding import PartitionSpec as P

EXPERTS_PER_NODE = 8
FEW_NODES = 8
COST = {"head": 100000000, "tail": 3000000000, "load": 30000000000, "join": 30000000000, "own": 100000000, "expert": 30000000000, "far0": 1, "far1": 10000000000, "fold": 1000000000, "final": 10000000000, "last": 30000000000}
PIECES = 4
HBM = pl.BlockSpec(memory_space=pltpu.HBM)
VMEM = pl.BlockSpec(memory_space=pltpu.VMEM)
SMEM = pl.BlockSpec(memory_space=pltpu.SMEM)
ROWS = (((0,), (0,)), ((), ()))
COLS = (((1,), (1,)), ((), ()))


def shift(value, axis, mask):
    size = lax.axis_size(axis)
    return lax.ppermute(value, axis, [(i, i ^ mask) for i in range(size)])


def over_nodes(pieces, known=()):
    count = len(pieces)
    known = known or [None] * count
    if count > FEW_NODES:
        moved = lax.all_to_all(jnp.stack(pieces), "node", split_axis=0, concat_axis=0, tiled=True)
        return [moved[n] for n in range(count)]
    moved = list(pieces)
    for m in range(count - 1, 0, -1):
        moved[m] = shift(pieces[m], "node", m) if known[m] is None else known[m]
    return moved


def dot(a, b, dims=(((1,), (0,)), ((), ()))):
    return lax.dot_general(a, b, dims, preferred_element_type=jnp.float32)


def bf16(value):
    return value.astype(jnp.bfloat16)


def struct(rows, cols, dtype=jnp.bfloat16):
    return jax.ShapeDtypeStruct((rows, cols), dtype)


def call(name, kernel, outs, args, specs=None, scratch=(), room=0, limit=0):
    if specs:
        args = [
            pltpu.with_memory_space_constraint(a, pltpu.HBM) if s is HBM else a
            for a, s in zip(args, specs)
        ]
    return pl.pallas_call(
        kernel,
        name="scope_" + name,
        out_shape=outs,
        in_specs=specs or [VMEM] * len(args),
        out_specs=jax.tree.map(lambda _: VMEM, outs),
        scratch_shapes=scratch,
        cost_estimate=pl.CostEstimate(flops=COST[name], bytes_accessed=0, transcendentals=0),
        compiler_params=pltpu.CompilerParams(vmem_limit_bytes=limit or (8 << 20) + room),
    )(*args)


def head_kernel(
    nodes, block, owner_ref, index_hbm, gate_hbm, tokens_hbm,
    first_ref, mix_ref, pick_ref, tokens_ref, index_ref, gate_ref, sems,
):
    copies = [
        pltpu.make_async_copy(index_hbm, index_ref, sems.at[0]),
        pltpu.make_async_copy(gate_hbm, gate_ref, sems.at[1]),
        pltpu.make_async_copy(tokens_hbm, tokens_ref, sems.at[2]),
    ]
    for copy in copies:
        copy.start()
    count, width = tokens_ref.shape
    head = first_ref.shape[0]
    row = lax.broadcasted_iota(jnp.int32, (count, count), 0)
    col = lax.broadcasted_iota(jnp.int32, (count, count), 1)
    earlier = bf16((row < col).astype(jnp.float32))
    copies[0].wait()
    copies[1].wait()
    index = index_ref[...]
    gates = gate_ref[...]
    chosen, weights = [], []
    for n in range(nodes):
        match = index == owner_ref[n]
        chosen.append(jnp.max(match.astype(jnp.float32), axis=0, keepdims=True))
        weights.append(jnp.sum(jnp.where(match, gates, 0.0), axis=0, keepdims=True))
    wanted = jnp.max(jnp.concatenate(chosen, axis=0), axis=0, keepdims=True)
    flags = jnp.concatenate(chosen + [wanted] + [jnp.zeros_like(wanted)] * (-(nodes + 1) % 8), axis=0)
    position = dot(bf16(flags), earlier)
    ahead = position[nodes : nodes + 1]
    total = jnp.sum(wanted)
    place = lax.broadcasted_iota(jnp.int32, (1, count), 1).astype(jnp.float32)
    rank = jnp.where(wanted > 0.5, ahead, total + place - ahead)
    order = bf16((rank == row.astype(jnp.float32)).astype(jnp.float32))
    slot = lax.broadcasted_iota(jnp.int32, (block, count), 0).astype(jnp.float32)
    picks, own, other = [], [], []
    for n in range(nodes):
        here = (position[n : n + 1] == slot) & (chosen[n] > 0.5)
        there = (position[n : n + 1] + block // 2 == slot) & (chosen[n] > 0.5)
        picks.append(here.astype(jnp.float32))
        own.append(jnp.where(here, weights[n], 0.0))
        other.append(jnp.where(there, weights[n], 0.0))
    own = jnp.concatenate(own, axis=0)
    other = jnp.concatenate(other, axis=0)
    own_high, other_high = bf16(own), bf16(other)
    own_low = bf16(own - own_high.astype(jnp.float32))
    other_low = bf16(other - other_high.astype(jnp.float32))
    slots = nodes * block
    mix_ref[:count] = order
    mix_ref[count : count + slots] = own_high
    mix_ref[count + slots :] = own_low
    pick_ref[...] = bf16(jnp.concatenate(picks, axis=0))
    first_ref[:, width : width + slots] = bf16(dot(order[:head], other_high, COLS))
    first_ref[:, width + slots :] = bf16(dot(order[:head], other_low, COLS))
    copies[2].wait()
    first_ref[:, :width] = bf16(dot(order[:head], tokens_ref[...]))


def tail_kernel(head, mix_ref, pick_ref, tokens_ref, near_ref, *rest):
    tokens = tokens_ref[...]
    for out in rest:
        out[...] = bf16(dot(mix_ref[head : head + out.shape[0]], tokens))
        head += out.shape[0]
    near_ref[...] = bf16(dot(pick_ref[...], tokens))


def last_kernel(start, mix_ref, tokens_ref, after_ref, out_ref):
    out_ref[...] = bf16(dot(mix_ref[start : start + out_ref.shape[0]], tokens_ref[...]))


def join_kernel(nodes, block, near_ref, first_ref, *outs):
    outs = outs[-nodes:]
    slots, width = near_ref.shape
    high = first_ref[:, width : width + slots].astype(jnp.float32)
    pick = bf16((high != 0.0).astype(jnp.float32))
    far = dot(pick, first_ref[:, :width], ROWS)
    both = near_ref[...].astype(jnp.float32) + far
    for n, out in enumerate(outs):
        out[...] = bf16(both[n * block : (n + 1) * block])


def mlp(rows, gate, up, down):
    v = dot(rows, gate[...])
    hidden = bf16(v / (1.0 + jnp.exp(-v)) * dot(rows, up[...]))
    return dot(hidden, down[...])


def load_kernel(gate_hbm, up_hbm, down_hbm, sg_hbm, su_hbm, near_ref, pack_ref, sg, su, sems):
    width, part = gate_hbm.shape
    copies = [(gate_hbm, 0), (up_hbm, width)]
    copies += [(down_hbm.at[:, i : i + part], 2 * width + i) for i in range(0, width, part)]
    copies = [
        pltpu.make_async_copy(
            source, pack_ref.at[place : place + source.shape[0]], sems.at[i]
        )
        for i, (source, place) in enumerate(copies)
    ]
    copies.append(pltpu.make_async_copy(sg_hbm, sg, sems.at[len(copies)]))
    copies.append(pltpu.make_async_copy(su_hbm, su, sems.at[len(copies)]))
    for copy in copies:
        copy.start()
    for copy in copies:
        copy.wait()


def expert_kernel(nodes, *refs):
    rows = [r[...] for r in refs[:nodes]]
    packs, outs = refs[nodes : nodes + 2], refs[nodes + 2 :]
    block, width = rows[0].shape
    half = block // 2
    part = packs[0].shape[1]
    rows = jnp.concatenate(rows, axis=0)
    hidden = []
    for pack in packs:
        v = dot(rows, pack[:width])
        hidden.append(bf16(v / (1.0 + jnp.exp(-v)) * dot(rows, pack[width : 2 * width])))
    for i in range(0, width, part):
        down = slice(2 * width + i, 2 * width + i + part)
        sums = dot(hidden[0], packs[0][down]) + dot(hidden[1], packs[1][down])
        start = 0
        for out in outs:
            size = out.shape[0]
            out[:, i : i + part] = bf16(sums[start : start + size])
            start += size


def blocks_of(refs, block, cols=slice(None)):
    pieces = []
    for r in refs:
        piece = r[:, cols].astype(jnp.float32)
        pieces += [piece] * (block // piece.shape[0])
    return bf16(jnp.concatenate(pieces, axis=0))


def own_kernel(tokens_ref, gate, up, down, after_ref, sg, su, sd_hbm, own_ref, sd, sem):
    copy = pltpu.make_async_copy(sd_hbm, sd, sem)
    copy.start()
    rows = tokens_ref[...]
    own_ref[...] = mlp(rows, gate, up, down)
    v = dot(rows, sg[...])
    hidden = bf16(v / (1.0 + jnp.exp(-v)) * dot(rows, su[...]))
    copy.wait()
    own_ref[...] += dot(hidden, sd[...])


def far_kernel(groups, *refs):
    ins, mats, outs = refs[:groups], refs[groups : groups + 6], refs[groups + 6 :]
    rows = jnp.concatenate([r[:, : outs[0].shape[1]] for r in ins], axis=0)
    sums = mlp(rows, *mats[:3]) + mlp(rows, *mats[3:])
    start = 0
    for out in outs:
        out[...] = sums[start : start + out.shape[0]].astype(out.dtype)
        start += out.shape[0]


def fold_kernel(block, part_ref, first_ref, *refs):
    width = part_ref.shape[1]
    replies = blocks_of(refs[:-1], block)
    slots = replies.shape[0]
    high = first_ref[:, width : width + slots]
    low = first_ref[:, width + slots :]
    refs[-1][...] = bf16(part_ref[...] + dot(high, replies) + dot(low, replies))


def final_kernel(block, back_count, *refs):
    own_ref, mix_ref = refs[:2]
    backs, replies = refs[2 : 2 + back_count], refs[2 + back_count : -3]
    out_hbm, out_ref, sems = refs[-3:]
    width = out_ref.shape[1]
    tile = width // PIECES
    copies = []
    for i in range(PIECES):
        cols = slice(i * tile, (i + 1) * tile)
        reply = blocks_of(replies, block, cols)
        terms = jnp.concatenate([*[r[:, cols] for r in backs], reply, reply], axis=0)
        out_ref[:, cols] = bf16(own_ref[:, cols] + dot(mix_ref[...], terms, ROWS))
        copies.append(pltpu.make_async_copy(out_ref.at[:, cols], out_hbm.at[:, cols], sems.at[i]))
        copies[-1].start()
    for copy in copies:
        copy.wait()


def per_device(
    tokens, routing_gate_weight, selected_expert_index, w_gate, w_up, w_down, s_gate, s_up, s_down
):
    nodes = lax.axis_size("node")
    count, width = tokens.shape
    capacity = count // 16
    block = 2 * capacity
    slots = nodes * block
    head = min(nodes * capacity, count)
    tail = count - head

    owners = jnp.arange(nodes, dtype=jnp.int32)
    if nodes <= FEW_NODES:
        owners = owners ^ lax.axis_index("node")
    topk = selected_expert_index.shape[1]
    first, mix, pick, held = call(
        "head",
        lambda *refs: head_kernel(nodes, block, *refs),
        (
            struct(head, width + 2 * slots),
            struct(count + 2 * slots, count),
            struct(slots, count),
            struct(count, width),
        ),
        (owners * EXPERTS_PER_NODE, selected_expert_index.T, routing_gate_weight.T, tokens),
        specs=[SMEM, HBM, HBM, HBM],
        scratch=[
            pltpu.VMEM((topk, count), jnp.int32),
            pltpu.VMEM((topk, count), jnp.float32),
            pltpu.SemaphoreType.DMA((3,)),
        ],
        limit=16 << 20,
    )
    far_first = shift(first, "local", 2)
    cut = tail * 4 // 6 // 16 * 16
    near, *rest = call(
        "tail",
        lambda *refs: tail_kernel(head, *refs),
        [struct(slots, width)] + [struct(cut, width)] * (cut > 0),
        (mix, pick, held),
        room=4 * (slots + count) * width,
    )
    rest_far = [shift(r, "local", 2) for r in rest]
    shared_mats = (s_gate, s_up, s_down)
    shared_far = [shift(w, "local", 1) for w in shared_mats]
    sent = call(
        "join",
        lambda *refs: join_kernel(nodes, block, *refs),
        [struct(block, width)] * nodes,
        (near, far_first, *[]),
        room=8 * slots * width,
    )
    part = w_gate.shape[2]
    pack, own_gate, own_up = call(
        "load",
        load_kernel,
        [struct(3 * width, part), struct(*s_gate.shape), struct(*s_up.shape)],
        (w_gate[0], w_up[0], w_down[0], s_gate, s_up, first),
        specs=[HBM] * 5 + [VMEM],
        scratch=[pltpu.SemaphoreType.DMA((4 + width // part,))],
        limit=16 << 20,
    )
    far_pack = shift(pack, "local", 1)
    arrived = over_nodes(sent)
    if tail > cut:
        last = call(
            "last",
            lambda *refs: last_kernel(head + cut, *refs),
            struct(tail - cut, width),
            (mix, held, sent[0]),
            room=4 * count * width,
        )
        rest_far.append(shift(last, "local", 2))
    own, own_down = call(
        "own",
        own_kernel,
        [struct(count, width, jnp.float32), struct(*s_down.shape)],
        (held, *shared_far, near, own_gate, own_up, s_down),
        specs=[VMEM] * 7 + [HBM],
        scratch=[pltpu.SemaphoreType.DMA],
        limit=16 << 20,
    )
    mats = [own_gate, own_up, own_down]
    whole = [n == 1 and nodes <= FEW_NODES for n in range(nodes)]
    replied = call(
        "expert",
        lambda *refs: expert_kernel(nodes, *refs),
        [
            struct(rows, width)
            for n in range(nodes)
            for rows in ([block] if whole[n] else [capacity] * 2)
        ],
        (*arrived, pack, far_pack),
        room=20 * slots * width + (4 << 20),
    )
    split = iter(replied)
    pairs = [[next(split)] if w else [next(split), next(split)] for w in whole]
    far_replies = over_nodes([p[-1] for p in pairs])
    replies = over_nodes([p[0] for p in pairs], [f if w else None for f, w in zip(far_replies, whole)])

    sums, late = [], []
    for i, rows in enumerate(([far_first] + rest_far[:1], rest_far[1:])):
        if rows:
            sums += call(
                "far" + str(i),
                lambda *refs, n=len(rows): far_kernel(n, *refs),
                [
                    struct(r.shape[0], width, jnp.float32 if r is far_first else jnp.bfloat16)
                    for r in rows
                ],
                (*rows, *shared_far, *mats),
                room=12 * count * width,
            )
    late = [shift(r, "local", 2) for r in sums[1:]]
    folded = call(
        "fold",
        lambda *refs: fold_kernel(block, *refs),
        struct(head, width),
        (sums[0], far_first, *far_replies),
        room=8 * slots * width,
    )
    backs = [shift(folded, "local", 2)] + late
    return pl.pallas_call(
        lambda *refs: final_kernel(block, len(backs), *refs),
        name="scope_final",
        out_shape=struct(count, width),
        in_specs=[VMEM] * (2 + len(backs) + nodes),
        out_specs=HBM,
        scratch_shapes=[
            pltpu.VMEM((count, width), jnp.bfloat16),
            pltpu.SemaphoreType.DMA((PIECES,)),
        ],
        cost_estimate=pl.CostEstimate(flops=COST["final"], bytes_accessed=0, transcendentals=0),
        compiler_params=pltpu.CompilerParams(vmem_limit_bytes=(8 << 20) + 8 * slots * width),
    )(own, mix, *backs, *replies)


def solution(mesh):
    in_specs = (
        P(("groups", "node", "local"), None),
        P(("groups", "node", "local"), None),
        P(("groups", "node", "local"), None),
        P("node", None, "local"),
        P("node", None, "local"),
        P("node", "local", None),
        P(None, "local"),
        P(None, "local"),
        P("local", None),
    )
    out_specs = P(("groups", "node", "local"), None)
    return jax.shard_map(
        per_device, mesh=mesh, in_specs=in_specs, out_specs=out_specs, check_vma=False
    )
```
